256 devices in a mesh: rows: 8 (over z_hi, core), pairs: 32 (over y, z_lo, x).
Axes of the slice: x: 4, y: 4, z: 8 (z_hi: 4, z_lo: 2; z = z_hi * 2 + z_lo), core: 2. Of those that a mesh axis runs over, the one named last changes fastest.
Arguments:
- snapshot: float32 [16384, 16384], P('rows', 'pairs'), may hold values from -60 to 60, as said below
- plan: int32 [3, 32], P(None, 'pairs'), may hold values from 0 to 1
Outputs:
- rotated_matrix: float32 [16384, 16384], P('rows', 'pairs')
The draws below stay inside these ranges and needn't reach their ends.
Inputs may be any that keep to these rules, and one draw needn't show every extreme that they name: `plan`: 1 says that the second held block moves on, 0 the first. `snapshot`: columns have scales of 1 to 10.
All inputs are finite; a program needn't handle non-finite values.
Results may differ from the reference program's by a relative error of at most 0.00012.
Values sent between devices are 32-bit elements; how exact they have to be, the bound alone decides.
A program may use at most 64 MiB of HBM per device.

```python
import math
import jax
import jax.numpy as jnp
from jax import lax

BLOCK = 256
STEPS = 3
ROWS = 16384
COLS = 16384
N_PAIRS = 32


def draw_snapshot(key, part):
    key = jax.random.fold_in(key, 1)
    first, second = jax.random.split(key, 2)
    scales = jnp.exp(jax.random.uniform(second, (COLS,), jnp.float32, 0.0, math.log(10.0)))
    values = jnp.clip(jax.random.normal(first, (ROWS, COLS), jnp.float32), -5.0, 5.0)
    return (values * scales[None, :]).astype(jnp.float32)


def with_ends(drawn, stream_key, low, top_value):
    place = [jax.random.randint(jax.random.fold_in(stream_key, axis), (), 0, length) for axis, length in enumerate(drawn.shape)]
    main_axis = drawn.shape.index(max(drawn.shape))
    beside = place[:main_axis] + [(place[main_axis] + 1) % drawn.shape[main_axis]] + place[main_axis + 1:]
    return drawn.at[tuple(place)].set(low).at[tuple(beside)].set(top_value)


def setup_inputs(seed: int = 0) -> dict:
    seeds = jax.random.split(jax.random.key(seed), 3)
    snapshot = draw_snapshot(jax.random.fold_in(seeds[2], 71), 0)
    plan = with_ends(jax.random.randint(seeds[1], (STEPS, N_PAIRS), 0, 2), jax.random.fold_in(seeds[1], 1), 0, 1).astype(jnp.int32)
    return dict(snapshot=snapshot, plan=plan)


epsilon = 1e-06

def polar_factor(cross, left_sq, right_sq):
    width = cross.shape[0]
    scaled = 0.5 * cross * lax.rsqrt(left_sq + epsilon)[:, None] * lax.rsqrt(right_sq + epsilon)[None, :]
    scaled = scaled / (1.0 + jnp.sqrt(jnp.sum(scaled * scaled)))
    zeros = jnp.zeros((width, width), jnp.float32)
    upper = jnp.concatenate([zeros, scaled], axis=1)
    lower = jnp.concatenate([-scaled.T, zeros], axis=1)
    rotation = (jnp.eye(2 * width, dtype=jnp.float32) + jnp.concatenate([upper, lower], axis=0)) / jnp.sqrt(jnp.float32(1.25))
    for sweep_iter in range(2):
        product = jnp.dot(rotation.T, rotation, precision=lax.Precision.HIGHEST)
        rotation = 1.5 * rotation - 0.5 * jnp.dot(rotation, product, precision=lax.Precision.HIGHEST)
    return rotation

def reference(snapshot, plan):
    current = snapshot.reshape(ROWS, N_PAIRS, 2, BLOCK)
    for sweep_step in range(STEPS):
        left_block = current[:, :, 0]
        right_block = current[:, :, 1]
        cross = jnp.einsum('mpa,mpb->pab', left_block, right_block, precision=lax.Precision.HIGHEST)
        left_sq = lax.optimization_barrier(jnp.sum(left_block * left_block, axis=0))
        right_sq = lax.optimization_barrier(jnp.sum(right_block * right_block, axis=0))
        rotation = jax.vmap(polar_factor)(cross, left_sq, right_sq)
        joined = current.reshape(ROWS, N_PAIRS, 2 * BLOCK)
        rotated = jnp.einsum('mpa,pab->mpb', joined, rotation, precision=lax.Precision.HIGHEST)
        chosen = (plan[sweep_step] == 1)[None, :, None]
        moving = jnp.where(chosen, rotated[:, :, BLOCK:], rotated[:, :, :BLOCK])
        staying = jnp.where(chosen, rotated[:, :, :BLOCK], rotated[:, :, BLOCK:])
        arrived = jnp.roll(moving, 1, axis=1)
        current = jnp.stack([staying, arrived], axis=2)
    return current.reshape(ROWS, COLS)
```

```python
import functools

import jax
import jax.numpy as jnp
from jax import lax
from jax.experimental import pallas as pl
from jax.experimental.pallas import tpu as pltpu
from jax.sharding import PartitionSpec as P
from numpy.polynomial import Polynomial

STEPS = 3
CHUNKS = 8
EPSILON = 1e-06
MESH = pl.DeviceIdType.MESH


def gains():
    product = Polynomial([0.8, 0.8])
    first = 1.5 - 0.5 * product
    second = 1.5 - 0.5 * product * first * first
    return [float(c) for c in (first * second / 1.25**0.5).coef]


def split(x):
    high = x.astype(jnp.bfloat16)
    return high, (x - high.astype(jnp.float32)).astype(jnp.bfloat16)


def dot(a, b, dims=(1, 0)):
    def one(x, y):
        return lax.dot_general(
            x, y, (((dims[0],), (dims[1],)), ((), ())), preferred_element_type=jnp.float32
        )

    return one(a[0], b[0]) + (one(a[0], b[1]) + one(a[1], b[0]))


def polynomial(square, eye, g):
    s = split(square)
    square2 = dot(s, s)
    return (g[0] * eye + g[1] * square + g[2] * square2) + dot(
        split(square2), split(g[3] * square + g[4] * square2)
    )


def kernel(
    n_pairs,
    snapshot,
    plan,
    out,
    data,
    staged,
    parted,
    partner_part,
    shares,
    arrived,
    cross,
    weights_high,
    weights_low,
    load_sem,
    pair_sem,
    share_sem,
    gather_sem,
    pass_sem,
    block_sem,
    last_sem,
):
    rows, width = snapshot.shape[0], snapshot.shape[1] // 2
    chunk, half, quarter = rows // CHUNKS, width // 2, width // 8
    r, p = lax.axis_index("rows"), lax.axis_index("pairs")
    core, z = lax.rem(r, 2), lax.div(r, 2)
    g = gains()

    def pair_at(distance):
        return lax.rem(p + distance + 2 * n_pairs, n_pairs)

    def chunk_rows(c):
        return pl.ds(pl.multiple_of(c * chunk, chunk), chunk)

    def row_at(c, z_index):
        return pl.ds(pl.multiple_of(c * half + z_index * quarter, quarter), quarter)

    def load(c, side):
        return pltpu.make_async_copy(
            snapshot.at[chunk_rows(c), pl.ds(side * width, width)],
            data.at[0, side, chunk_rows(c)],
            load_sem.at[c, side],
        )

    for c in range(CHUNKS):
        for side in range(2):
            load(c, side).start()

    barrier = pltpu.get_barrier_semaphore()
    peers = [(lax.rem(z + j, 4) * 2 + core, p) for j in (1, 2, 3)]
    peers += [(r, pair_at(d)) for d in (1, -1, 2, -2, 3, -3)]
    peers += [(z * 2 + 1 - core, pair_at(d)) for d in (0, 1, -1, 2, -2)]
    for peer in peers:
        pl.semaphore_signal(barrier, inc=1, device_id=peer, device_id_type=MESH)

    def remote(src, dst, sems, device):
        return pltpu.make_async_remote_copy(
            src_ref=src,
            dst_ref=dst,
            send_sem=sems.at[0],
            recv_sem=sems.at[1],
            device_id=device,
            device_id_type=MESH,
        )

    eye = (
        lax.broadcasted_iota(jnp.int32, (width, width), 0)
        == lax.broadcasted_iota(jnp.int32, (width, width), 1)
    ).astype(jnp.float32)

    def sent(step, c):
        return remote(
            staged.at[0, chunk_rows(c)],
            data.at[step + 1, 1 - core, chunk_rows(c)],
            block_sem.at[step, c],
            (r, pair_at(1 - 2 * core)),
        )

    def last_first(c):
        return remote(
            staged.at[0, chunk_rows(c)],
            out.at[chunk_rows(c), pl.ds(pl.multiple_of((1 - core) * width, width), width)],
            block_sem.at[STEPS - 1, c],
            (r, pair_at(1 + core)),
        )

    def last_second(c):
        return remote(
            staged.at[1, chunk_rows(c)],
            out.at[chunk_rows(c), pl.ds(width, width)],
            last_sem.at[c],
            (r, pair_at(3)),
        )

    def last_local(c):
        return pltpu.make_async_copy(
            staged.at[1, chunk_rows(c)],
            out.at[chunk_rows(c), pl.ds(0, width)],
            last_sem.at[c, 0],
        )

    for step in range(STEPS):
        parted[step] = jnp.zeros(parted.shape[1:], jnp.float32)

        @pl.loop(0, CHUNKS)
        def _(c):
            if step == 0:
                load(c, 0).wait()
                load(c, 1).wait()
            else:
                sent(step - 1, c).wait_recv()
            left = data[step, 0, chunk_rows(c)]
            right = data[step, 1, chunk_rows(c)]
            product = dot(split(left), split(right), (0, 0))
            parted[step, 0, :half] += product[:half]
            parted[step, 1, :half] += product[half:]
            parted[step, 0, half : half + 1] += jnp.sum(left * left, axis=0, keepdims=True)
            parted[step, 0, half + 1 : half + 2] += jnp.sum(right * right, axis=0, keepdims=True)

        choice = plan[step, 0].astype(jnp.float32) * (1 - core).astype(jnp.float32)
        parted[step, 0, half + 2 : half + 3] = jnp.full((1, width), 1.0, jnp.float32) * choice
        parted[step, 1, half:] = parted[step, 0, half:]

        if step == 0:
            pl.semaphore_wait(barrier, len(peers))

        partner = (z * 2 + 1 - core, pair_at(step * (2 * core - 1)))
        exchange = remote(
            parted.at[step, 1 - core], partner_part.at[step], pair_sem.at[step], partner
        )
        exchange.start()
        exchange.wait_recv()
        for k in range(4):
            at = slice(k * quarter, (k + 1) * quarter)
            shares[step, k, :quarter] = parted[step, core, at] + partner_part[step, at]
            shares[step, k, quarter:] = parted[step, core, half:] + partner_part[step, half:]

        def share(j):
            k = lax.rem(z + j, 4)
            return remote(
                shares.at[step, k], arrived.at[step, z], share_sem.at[step, j], (k * 2 + core, p)
            )

        def share_in(j):
            return remote(
                shares.at[step, z],
                arrived.at[step, lax.rem(z + 4 - j, 4)],
                share_sem.at[step, j],
                (r, pair_at(1)),
            )

        for j in (2, 1, 3):
            share(j).start()
        arrived[step, z] = shares[step, z]
        for j in (1, 3, 2):
            share_in(j).wait_recv()
        total = (arrived[step, 0] + arrived[step, 1]) + (arrived[step, 2] + arrived[step, 3])
        mine = row_at(core, z)
        cross[step, mine] = total[:quarter]

        def gather(j):
            return remote(
                cross.at[step, mine],
                cross.at[step, mine],
                gather_sem.at[step, j],
                (lax.rem(z + j, 4) * 2 + core, p),
            )

        def gather_in(j):
            at = row_at(core, lax.rem(z + 4 - j, 4))
            return remote(
                cross.at[step, at], cross.at[step, at], gather_sem.at[step, j], (r, pair_at(1))
            )

        def passed(j):
            at = row_at(core, lax.rem(z + 4 - j, 4))
            return remote(cross.at[step, at], cross.at[step, at], pass_sem.at[step, j], partner)

        def passed_in(j):
            at = row_at(1 - core, lax.rem(z + 4 - j, 4))
            return remote(cross.at[step, at], cross.at[step, at], pass_sem.at[step, j], partner)

        for j in (2, 1, 3):
            gather(j).start()
        passed(0).start()
        for j in (1, 3, 2):
            gather_in(j).wait_recv()
            passed(j).start()

        squares = total[quarter:]
        left_scale = lax.rsqrt(squares[0:1] + EPSILON)
        right_scale = lax.rsqrt(squares[1:2] + EPSILON)
        left_scale = jnp.broadcast_to(left_scale, (width, width)).T
        for j in range(4):
            passed_in(j).wait_recv()

        scaled = 0.5 * cross[step] * left_scale * right_scale
        scaled = scaled / (1.0 + jnp.sqrt(jnp.sum(scaled * scaled)))
        e = split(scaled)
        upper = polynomial(dot(e, e, (1, 1)), eye, g)
        lower = polynomial(dot(e, e, (0, 0)), eye, g)
        mixed = dot(split(upper), e)
        turned = -mixed.T
        chosen = squares[2:3] * 0.25
        flip = core.astype(jnp.float32)
        second_sent = (chosen * (1.0 - flip) + (1.0 - chosen) * flip) > 0.5
        for at, zero, one in (
            (slice(0, width), upper, mixed),
            (slice(width, 2 * width), turned, lower),
        ):
            kept_high, kept_low = split(jnp.where(second_sent, zero, one))
            sent_high, sent_low = split(jnp.where(second_sent, one, zero))
            weights_high[at, :width] = kept_high
            weights_high[at, width:] = sent_high
            weights_low[at, :width] = kept_low
            weights_low[at, width:] = sent_low

        if step > 0:

            @pl.loop(0, CHUNKS)
            def _(c):
                sent(step - 1, c).wait_send()

        @pl.loop(0, CHUNKS)
        def _(c):
            at = chunk_rows(c)
            high, low = split(jnp.concatenate([data[step, 0, at], data[step, 1, at]], axis=1))
            result = dot((high, low), (weights_high[...], weights_low[...]))
            staged[0, at] = result[:, width:]
            if step < STEPS - 1:
                sent(step, c).start()
                data[step + 1, core, at] = result[:, :width]
            else:
                last_first(c).start()
                staged[1, at] = result[:, :width]

                @pl.when(core == 0)
                def _():
                    last_local(c).start()

                @pl.when(core == 1)
                def _():
                    last_second(c).start()

        exchange.wait_send()
        for j in (1, 2, 3):
            share(j).wait_send()
            gather(j).wait_send()
        for j in range(4):
            passed(j).wait_send()

    @pl.loop(0, CHUNKS)
    def _(c):
        last_first(c).wait()

        @pl.when(core == 0)
        def _():
            last_local(c).wait()

        @pl.when(core == 1)
        def _():
            last_second(c).wait()


def body(snapshot, plan):
    rows, width = snapshot.shape[0], snapshot.shape[1] // 2
    half, quarter = width // 2, width // 8
    dma = pltpu.SemaphoreType.DMA
    f32 = jnp.float32
    return pl.pallas_call(
        functools.partial(kernel, lax.axis_size("pairs")),
        out_shape=jax.ShapeDtypeStruct(snapshot.shape, f32),
        in_specs=[
            pl.BlockSpec(memory_space=pl.ANY),
            pl.BlockSpec(memory_space=pltpu.SMEM),
        ],
        out_specs=pl.BlockSpec(memory_space=pl.ANY),
        scratch_shapes=[
            pltpu.VMEM((STEPS, 2, rows, width), f32),
            pltpu.VMEM((2, rows, width), f32),
            pltpu.VMEM((STEPS, 2, half + 8, width), f32),
            pltpu.VMEM((STEPS, half + 8, width), f32),
            pltpu.VMEM((STEPS, 4, quarter + 8, width), f32),
            pltpu.VMEM((STEPS, 4, quarter + 8, width), f32),
            pltpu.VMEM((STEPS, width, width), f32),
            pltpu.VMEM((2 * width, 2 * width), jnp.bfloat16),
            pltpu.VMEM((2 * width, 2 * width), jnp.bfloat16),
            dma((CHUNKS, 2)),
            dma((STEPS, 2)),
            dma((STEPS, 4, 2)),
            dma((STEPS, 4, 2)),
            dma((STEPS, 4, 2)),
            dma((STEPS, CHUNKS, 2)),
            dma((CHUNKS, 2)),
        ],
        compiler_params=pltpu.CompilerParams(
            collective_id=0, has_side_effects=True, vmem_limit_bytes=44 * 1024 * 1024
        ),
    )(snapshot, plan)


def solution(mesh):
    placed = (P("rows", "pairs"), P(None, "pairs"))
    return jax.shard_map(
        body, mesh=mesh, in_specs=placed, out_specs=P("rows", "pairs"), check_vma=False
    )
```

```python
import functools

import jax
import jax.numpy as jnp
from jax import lax
from jax.experimental import pallas as pl
from jax.experimental.pallas import tpu as pltpu
from jax.sharding import PartitionSpec as P
from numpy.polynomial import Polynomial

STEPS = 3
CHUNKS = 8
LINE = 4
EPSILON = 1e-06
MESH = pl.DeviceIdType.MESH


def gains():
    product = Polynomial([0.8, 0.8])
    first = 1.5 - 0.5 * product
    second = 1.5 - 0.5 * product * first * first
    return [float(c) for c in (first * second / 1.25**0.5).coef]


def split(x):
    high = x.astype(jnp.bfloat16)
    return high, (x - high.astype(jnp.float32)).astype(jnp.bfloat16)


def dot(a, b, dims=(1, 0)):
    def one(x, y):
        return lax.dot_general(
            x, y, (((dims[0],), (dims[1],)), ((), ())), preferred_element_type=jnp.float32
        )

    return one(a[0], b[0]) + (one(a[0], b[1]) + one(a[1], b[0]))


def polynomial(square, eye, g):
    s = split(square)
    square2 = dot(s, s)
    return (g[0] * eye + g[1] * square + g[2] * square2) + dot(
        split(square2), split(g[3] * square + g[4] * square2)
    )


def kernel(
    n_pairs,
    snapshot,
    plan,
    out,
    data,
    staged,
    relayed,
    squares,
    parted,
    partner_part,
    shares,
    arrived,
    cross,
    weights_high,
    weights_low,
    load_sem,
    square_sem,
    pair_sem,
    share_sem,
    gather_sem,
    pass_sem,
    block_sem,
    staying_sem,
    moving_sem,
    relay_sem,
):
    rows, width = snapshot.shape[0], snapshot.shape[1] // 2
    chunk, half, quarter = rows // CHUNKS, width // 2, width // 8
    r, p = lax.axis_index("rows"), lax.axis_index("pairs")
    core, z, x = lax.rem(r, 2), lax.div(r, 2), lax.rem(p, LINE)
    g = gains()

    def pair_at(distance):
        return lax.rem(p + distance + 2 * n_pairs, n_pairs)

    def chunk_rows(c):
        return pl.ds(pl.multiple_of(c * chunk, chunk), chunk)

    def row_at(c, z_index):
        return pl.ds(pl.multiple_of(c * half + z_index * quarter, quarter), quarter)

    def load(c, side):
        return pltpu.make_async_copy(
            snapshot.at[chunk_rows(c), pl.ds(side * width, width)],
            data.at[0, side, chunk_rows(c)],
            load_sem.at[c, side],
        )

    for c in range(CHUNKS):
        for side in range(2):
            load(c, side).start()

    barrier = pltpu.get_barrier_semaphore()
    peers = [(lax.rem(z + j, 4) * 2 + core, p) for j in (1, 2, 3)]
    peers += [(r, pair_at(d)) for d in (1, -1, 2, -2, 3, -3, 4, -4)]
    peers += [
        (lax.rem(z + j, 4) * 2 + 1 - core, pair_at(step * (2 * core - 1)))
        for j in range(4)
        for step in range(STEPS)
    ]
    for peer in peers:
        pl.semaphore_signal(barrier, inc=1, device_id=peer, device_id_type=MESH)

    def remote(src, dst, sems, device):
        return pltpu.make_async_remote_copy(
            src_ref=src,
            dst_ref=dst,
            send_sem=sems.at[0],
            recv_sem=sems.at[1],
            device_id=device,
            device_id_type=MESH,
        )

    eye = (
        lax.broadcasted_iota(jnp.int32, (width, width), 0)
        == lax.broadcasted_iota(jnp.int32, (width, width), 1)
    ).astype(jnp.float32)

    def sent(step, c):
        return remote(
            staged.at[0, chunk_rows(c)],
            data.at[step + 1, 1 - core, chunk_rows(c)],
            block_sem.at[step, c],
            (r, pair_at(1 - 2 * core)),
        )

    first_half, second_half = pl.ds(0, width), pl.ds(width, width)
    detours = jnp.where(core == 0, x == LINE - 1, x != 0)
    relays = jnp.where(core == 0, x == 0, x != 0)

    def staying_local(c):
        return pltpu.make_async_copy(
            staged.at[0, chunk_rows(c)], out.at[chunk_rows(c), first_half], staying_sem.at[c, 0]
        )

    def staying_back(c):
        return remote(
            staged.at[0, chunk_rows(c)],
            out.at[chunk_rows(c), first_half],
            staying_sem.at[c],
            (r, pair_at(2)),
        )

    def moving_direct(c):
        return remote(
            staged.at[1, chunk_rows(c)],
            out.at[chunk_rows(c), second_half],
            moving_sem.at[c],
            (r, pair_at(1 + 2 * core)),
        )

    def moving_detour(c):
        return pltpu.make_async_remote_copy(
            src_ref=staged.at[1, chunk_rows(c)],
            dst_ref=relayed.at[chunk_rows(c)],
            send_sem=moving_sem.at[c, 0],
            recv_sem=relay_sem.at[c, 1],
            device_id=(r, pair_at(7 * core - 3)),
            device_id_type=MESH,
        )

    def relay(c):
        return pltpu.make_async_remote_copy(
            src_ref=relayed.at[chunk_rows(c)],
            dst_ref=out.at[chunk_rows(c), second_half],
            send_sem=relay_sem.at[c, 0],
            recv_sem=moving_sem.at[c, 1],
            device_id=(r, pair_at(4 - 5 * core)),
            device_id_type=MESH,
        )

    for step in range(STEPS):
        parted[step] = jnp.zeros((width, width), jnp.float32)
        slot = z * 2 + core
        squares[step, slot] = jnp.zeros((1, 2 * width + 128), jnp.float32)

        @pl.loop(0, CHUNKS)
        def _(c):
            if step == 0:
                load(c, 0).wait()
                load(c, 1).wait()
            else:
                sent(step - 1, c).wait_recv()
            left = data[step, 0, chunk_rows(c)]
            right = data[step, 1, chunk_rows(c)]
            parted[step] += dot(split(left), split(right), (0, 0))
            squares[step, slot, :, :width] += jnp.sum(left * left, axis=0, keepdims=True)
            squares[step, slot, :, width : 2 * width] += jnp.sum(
                right * right, axis=0, keepdims=True
            )

        choice = plan[step : step + 1, :].astype(jnp.float32) * (1 - core).astype(jnp.float32)
        squares[step, slot, :, 2 * width :] = jnp.broadcast_to(choice, (1, 128))

        if step == 0:
            pl.semaphore_wait(barrier, len(peers))

        partner_pair = pair_at(step * (2 * core - 1))
        partner = (z * 2 + 1 - core, partner_pair)

        def exchange(j):
            k = lax.rem(z + j, 4)
            return remote(
                parted.at[step, row_at(1 - core, k)],
                partner_part.at[step, k],
                pair_sem.at[step, j],
                partner,
            )

        def square(j):
            other = lax.rem(slot + j, 8)
            same = lax.rem(other, 2) == core
            return remote(
                squares.at[step, slot],
                squares.at[step, slot],
                square_sem.at[step, j],
                (other, jnp.where(same, p, partner_pair)),
            )

        def square_in(j):
            at = squares.at[step, lax.rem(slot + 8 - j, 8)]
            return remote(at, at, square_sem.at[step, j], partner)

        for j in (2, 1, 3, 0):
            exchange(j).start()
        for j in range(1, 8):
            square(j).start()

        def share(j):
            k = lax.rem(z + j, 4)
            return remote(
                shares.at[step, k], arrived.at[step, z], share_sem.at[step, j], (k * 2 + core, p)
            )

        def share_in(j):
            return remote(
                shares.at[step, z],
                arrived.at[step, lax.rem(z + 4 - j, 4)],
                share_sem.at[step, j],
                (r, pair_at(1)),
            )

        for j in (2, 1, 3, 0):
            k = lax.rem(z + j, 4)
            exchange(j).wait_recv()
            own = parted[step, row_at(core, k)] + partner_part[step, k]
            if j:
                shares[step, k] = own
                share(j).start()
            else:
                arrived[step, k] = own
        for j in (1, 3, 2):
            share_in(j).wait_recv()
        mine = row_at(core, z)
        cross[step, mine] = (arrived[step, 0] + arrived[step, 1]) + (
            arrived[step, 2] + arrived[step, 3]
        )

        def gather(j):
            return remote(
                cross.at[step, mine],
                cross.at[step, mine],
                gather_sem.at[step, j],
                (lax.rem(z + j, 4) * 2 + core, p),
            )

        def gather_in(j):
            at = row_at(core, lax.rem(z + 4 - j, 4))
            return remote(
                cross.at[step, at], cross.at[step, at], gather_sem.at[step, j], (r, pair_at(1))
            )

        def passed(j):
            at = row_at(core, lax.rem(z + 4 - j, 4))
            return remote(cross.at[step, at], cross.at[step, at], pass_sem.at[step, j], partner)

        def passed_in(j):
            at = row_at(1 - core, lax.rem(z + 4 - j, 4))
            return remote(cross.at[step, at], cross.at[step, at], pass_sem.at[step, j], partner)

        for j in (2, 1, 3):
            gather(j).start()
        passed(0).start()
        for j in (1, 3, 2):
            gather_in(j).wait_recv()
            passed(j).start()

        for j in range(1, 8):
            square_in(j).wait_recv()
        total = squares[step, 0]
        for k in range(1, 8):
            total = total + squares[step, k]
        left_scale = lax.rsqrt(total[:, :width] + EPSILON)
        right_scale = lax.rsqrt(total[:, width : 2 * width] + EPSILON)
        left_scale = jnp.broadcast_to(left_scale, (width, width)).T
        for j in range(4):
            passed_in(j).wait_recv()

        scaled = 0.5 * cross[step] * left_scale * right_scale
        scaled = scaled / (1.0 + jnp.sqrt(jnp.sum(scaled * scaled)))
        e = split(scaled)
        upper = polynomial(dot(e, e, (1, 1)), eye, g)
        lower = polynomial(dot(e, e, (0, 0)), eye, g)
        mixed = dot(split(upper), e)
        turned = -mixed.T
        chosen = jnp.concatenate([total[:, 2 * width :]] * (width // 128), axis=1) * 0.25
        flip = core.astype(jnp.float32) if step < STEPS - 1 else 0.0
        second_sent = (chosen * (1.0 - flip) + (1.0 - chosen) * flip) > 0.5
        for at, zero, one in (
            (slice(0, width), upper, mixed),
            (slice(width, 2 * width), turned, lower),
        ):
            kept_high, kept_low = split(jnp.where(second_sent, zero, one))
            sent_high, sent_low = split(jnp.where(second_sent, one, zero))
            weights_high[at, :width] = kept_high
            weights_high[at, width:] = sent_high
            weights_low[at, :width] = kept_low
            weights_low[at, width:] = sent_low

        if step > 0:

            @pl.loop(0, CHUNKS)
            def _(c):
                sent(step - 1, c).wait_send()

        @pl.loop(0, CHUNKS)
        def _(c):
            at = chunk_rows(c)
            high, low = split(jnp.concatenate([data[step, 0, at], data[step, 1, at]], axis=1))
            result = dot((high, low), (weights_high[...], weights_low[...]))
            if step < STEPS - 1:
                staged[0, at] = result[:, width:]
                sent(step, c).start()
                data[step + 1, core, at] = result[:, :width]
            else:
                staged[1, at] = result[:, width:]

                @pl.when(detours)
                def _():
                    moving_detour(c).start()

                @pl.when(jnp.logical_not(detours))
                def _():
                    moving_direct(c).start()

                staged[0, at] = result[:, :width]

                @pl.when(core == 0)
                def _():
                    staying_local(c).start()

                @pl.when(core == 1)
                def _():
                    staying_back(c).start()

        for j in range(4):
            exchange(j).wait_send()
            passed(j).wait_send()
        for j in (1, 2, 3):
            share(j).wait_send()
            gather(j).wait_send()
        for j in range(1, 8):
            square(j).wait_send()

    @pl.when(relays)
    def _():
        @pl.loop(0, CHUNKS)
        def _(c):
            moving_detour(c).wait_recv()
            relay(c).start()

    @pl.loop(0, CHUNKS)
    def _(c):
        moving_direct(c).wait()

        @pl.when(relays)
        def _():
            relay(c).wait_send()

        @pl.when(core == 0)
        def _():
            staying_local(c).wait()

        @pl.when(core == 1)
        def _():
            staying_back(c).wait()


def body(snapshot, plan):
    rows, width = snapshot.shape[0], snapshot.shape[1] // 2
    quarter = width // 8
    dma = pltpu.SemaphoreType.DMA
    f32 = jnp.float32
    return pl.pallas_call(
        functools.partial(kernel, lax.axis_size("pairs")),
        out_shape=jax.ShapeDtypeStruct(snapshot.shape, f32),
        in_specs=[
            pl.BlockSpec(memory_space=pl.ANY),
            pl.BlockSpec(memory_space=pltpu.VMEM),
        ],
        out_specs=pl.BlockSpec(memory_space=pl.ANY),
        scratch_shapes=[
            pltpu.VMEM((STEPS, 2, rows, width), f32),
            pltpu.VMEM((2, rows, width), f32),
            pltpu.VMEM((rows, width), f32),
            pltpu.VMEM((STEPS, 8, 1, 2 * width + 128), f32),
            pltpu.VMEM((STEPS, width, width), f32),
            pltpu.VMEM((STEPS, 4, quarter, width), f32),
            pltpu.VMEM((STEPS, 4, quarter, width), f32),
            pltpu.VMEM((STEPS, 4, quarter, width), f32),
            pltpu.VMEM((STEPS, width, width), f32),
            pltpu.VMEM((2 * width, 2 * width), jnp.bfloat16),
            pltpu.VMEM((2 * width, 2 * width), jnp.bfloat16),
            dma((CHUNKS, 2)),
            dma((STEPS, 8, 2)),
            dma((STEPS, 4, 2)),
            dma((STEPS, 4, 2)),
            dma((STEPS, 4, 2)),
            dma((STEPS, 4, 2)),
            dma((STEPS, CHUNKS, 2)),
            dma((CHUNKS, 2)),
            dma((CHUNKS, 2)),
            dma((CHUNKS, 2)),
        ],
        compiler_params=pltpu.CompilerParams(
            collective_id=0, has_side_effects=True, vmem_limit_bytes=60 * 1024 * 1024
        ),
    )(snapshot, plan)


def solution(mesh):
    placed = (P("rows", "pairs"), P(None, "pairs"))
    return jax.shard_map(
        body, mesh=mesh, in_specs=placed, out_specs=P("rows", "pairs"), check_vma=False
    )
```

```python
import functools

import jax
import jax.numpy as jnp
from jax import lax
from jax.experimental import pallas as pl
from jax.experimental.pallas import tpu as pltpu
from jax.sharding import PartitionSpec as P
from numpy.polynomial import Polynomial

STEPS = 3
CHUNKS = 8
LINE = 4
EPSILON = 1e-06
MESH = pl.DeviceIdType.MESH


def gains():
    product = Polynomial([0.8, 0.8])
    first = 1.5 - 0.5 * product
    second = 1.5 - 0.5 * product * first * first
    return [float(c) for c in (first * second / 1.25**0.5).coef]


def split(x):
    high = x.astype(jnp.bfloat16)
    return high, (x - high.astype(jnp.float32)).astype(jnp.bfloat16)


def dot(a, b, dims=(1, 0)):
    def one(x, y):
        return lax.dot_general(
            x, y, (((dims[0],), (dims[1],)), ((), ())), preferred_element_type=jnp.float32
        )

    return one(a[0], b[0]) + (one(a[0], b[1]) + one(a[1], b[0]))


def polynomial(square, eye, g):
    s = split(square)
    square2 = dot(s, s)
    return (g[0] * eye + g[1] * square + g[2] * square2) + dot(
        split(square2), split(g[3] * square + g[4] * square2)
    )


def kernel(
    n_pairs,
    snapshot,
    plan,
    out,
    data,
    staged,
    relayed,
    squares,
    parted,
    partner_part,
    shares,
    arrived,
    cross,
    weights_high,
    weights_low,
    load_sem,
    square_sem,
    pair_sem,
    share_sem,
    gather_sem,
    pass_sem,
    block_sem,
    staying_sem,
    moving_sem,
    relay_sem,
):
    rows, width = snapshot.shape[0], snapshot.shape[1] // 2
    chunk, half, quarter = rows // CHUNKS, width // 2, width // 8
    r, p = lax.axis_index("rows"), lax.axis_index("pairs")
    core, z, x = lax.rem(r, 2), lax.div(r, 2), lax.rem(p, LINE)
    g = gains()

    def pair_at(distance):
        return lax.rem(p + distance + 2 * n_pairs, n_pairs)

    def chunk_rows(c):
        return pl.ds(pl.multiple_of(c * chunk, chunk), chunk)

    def row_at(c, z_index):
        return pl.ds(pl.multiple_of(c * half + z_index * quarter, quarter), quarter)

    def load(c, side):
        return pltpu.make_async_copy(
            snapshot.at[chunk_rows(c), pl.ds(side * width, width)],
            data.at[0, side, chunk_rows(c)],
            load_sem.at[c, side],
        )

    for c in range(CHUNKS):
        for side in range(2):
            load(c, side).start()

    barrier = pltpu.get_barrier_semaphore()
    peers = [(lax.rem(z + j, 4) * 2 + core, p) for j in (1, 2, 3)]
    peers += [(r, pair_at(d)) for d in (1, -1, 2, -2, 3, -3, 4, -4)]
    peers += [
        (lax.rem(z + j, 4) * 2 + 1 - core, pair_at(step * (2 * core - 1)))
        for j in range(4)
        for step in range(STEPS)
    ]
    for peer in peers:
        pl.semaphore_signal(barrier, inc=1, device_id=peer, device_id_type=MESH)

    def remote(src, dst, sems, device):
        return pltpu.make_async_remote_copy(
            src_ref=src,
            dst_ref=dst,
            send_sem=sems.at[0],
            recv_sem=sems.at[1],
            device_id=device,
            device_id_type=MESH,
        )

    eye = (
        lax.broadcasted_iota(jnp.int32, (width, width), 0)
        == lax.broadcasted_iota(jnp.int32, (width, width), 1)
    ).astype(jnp.float32)

    def sent(step, c):
        return remote(
            staged.at[0, chunk_rows(c)],
            data.at[step + 1, 1 - core, chunk_rows(c)],
            block_sem.at[step, c],
            (r, pair_at(1 - 2 * core)),
        )

    first_half, second_half = pl.ds(0, width), pl.ds(width, width)
    detours = jnp.where(core == 0, x == LINE - 1, x != 0)
    relays = jnp.where(core == 0, x == 0, x != 0)

    def staying_local(c):
        return pltpu.make_async_copy(
            staged.at[0, chunk_rows(c)], out.at[chunk_rows(c), first_half], staying_sem.at[c, 0]
        )

    def staying_back(c):
        return remote(
            staged.at[0, chunk_rows(c)],
            out.at[chunk_rows(c), first_half],
            staying_sem.at[c],
            (r, pair_at(2)),
        )

    def moving_direct(c):
        return remote(
            staged.at[1, chunk_rows(c)],
            out.at[chunk_rows(c), second_half],
            moving_sem.at[c],
            (r, pair_at(1 + 2 * core)),
        )

    def moving_detour(c):
        return pltpu.make_async_remote_copy(
            src_ref=staged.at[1, chunk_rows(c)],
            dst_ref=relayed.at[chunk_rows(c)],
            send_sem=moving_sem.at[c, 0],
            recv_sem=relay_sem.at[c, 1],
            device_id=(r, pair_at(7 * core - 3)),
            device_id_type=MESH,
        )

    def relay(c):
        return pltpu.make_async_remote_copy(
            src_ref=relayed.at[chunk_rows(c)],
            dst_ref=out.at[chunk_rows(c), second_half],
            send_sem=relay_sem.at[c, 0],
            recv_sem=moving_sem.at[c, 1],
            device_id=(r, pair_at(4 - 5 * core)),
            device_id_type=MESH,
        )

    for step in range(STEPS):
        parted[step] = jnp.zeros((width, width), jnp.float32)
        slot = z * 2 + core
        squares[step, slot] = jnp.zeros((1, 2 * width + 128), jnp.float32)

        @pl.loop(0, CHUNKS)
        def _(c):
            if step == 0:
                load(c, 0).wait()
                load(c, 1).wait()
            else:
                sent(step - 1, c).wait_recv()
            left = data[step, 0, chunk_rows(c)]
            right = data[step, 1, chunk_rows(c)]
            parted[step] += dot(split(left), split(right), (0, 0))
            squares[step, slot, :, :width] += jnp.sum(left * left, axis=0, keepdims=True)
            squares[step, slot, :, width : 2 * width] += jnp.sum(
                right * right, axis=0, keepdims=True
            )

        choice = plan[step : step + 1, :].astype(jnp.float32) * (1 - core).astype(jnp.float32)
        squares[step, slot, :, 2 * width :] = jnp.broadcast_to(choice, (1, 128))

        if step == 0:
            pl.semaphore_wait(barrier, len(peers))

        partner_pair = pair_at(step * (2 * core - 1))
        partner = (z * 2 + 1 - core, partner_pair)

        def exchange(j):
            k = lax.rem(z + j, 4)
            return remote(
                parted.at[step, row_at(1 - core, k)],
                partner_part.at[step, k],
                pair_sem.at[step, j],
                partner,
            )

        def square(j):
            other = lax.rem(slot + j, 8)
            same = lax.rem(other, 2) == core
            return remote(
                squares.at[step, slot],
                squares.at[step, slot],
                square_sem.at[step, j],
                (other, jnp.where(same, p, partner_pair)),
            )

        def square_in(j):
            at = squares.at[step, lax.rem(slot + 8 - j, 8)]
            return remote(at, at, square_sem.at[step, j], partner)

        far = lax.rem(z + 2, 4)

        def far_share(t):
            to = core if t == 0 else 1 - core
            return remote(
                parted.at[step, row_at(to, far)],
                arrived.at[step, z if t == 0 else 4],
                share_sem.at[step, 2 * t],
                (far * 2 + to, p if t == 0 else partner_pair),
            )

        def far_share_in(t):
            at = arrived.at[step, far if t == 0 else 4]
            return remote(at, at, share_sem.at[step, 2 * t], partner)

        far_share(0).start()
        far_share(1).start()
        for j in (1, 3, 0):
            exchange(j).start()
        for j in range(1, 8):
            square(j).start()

        def share(j):
            k = lax.rem(z + j, 4)
            return remote(
                shares.at[step, j], arrived.at[step, z], share_sem.at[step, j], (k * 2 + core, p)
            )

        def share_in(j):
            at = arrived.at[step, lax.rem(z + 4 - j, 4)]
            return remote(at, at, share_sem.at[step, j], partner)

        for j in (1, 3, 0):
            k = lax.rem(z + j, 4)
            exchange(j).wait_recv()
            own = parted[step, row_at(core, k)] + partner_part[step, k]
            if j:
                shares[step, j] = own
                share(j).start()
            else:
                arrived[step, k] = own
        for j in (1, 3):
            share_in(j).wait_recv()
        far_share_in(0).wait_recv()
        far_share_in(1).wait_recv()
        mine = row_at(core, z)
        cross[step, mine] = (arrived[step, 0] + arrived[step, 1]) + (
            (arrived[step, 2] + arrived[step, 3]) + arrived[step, 4]
        )

        def gather(j):
            return remote(
                cross.at[step, mine],
                cross.at[step, mine],
                gather_sem.at[step, j],
                (lax.rem(z + j, 4) * 2 + core, p),
            )

        def gather_in(j):
            at = row_at(core, lax.rem(z + 4 - j, 4))
            return remote(
                cross.at[step, at], cross.at[step, at], gather_sem.at[step, j], (r, pair_at(1))
            )

        def passed(j):
            at = row_at(core, lax.rem(z + 4 - j, 4) if j != 2 else z)
            to = partner if j != 2 else (far * 2 + 1 - core, partner_pair)
            return remote(cross.at[step, at], cross.at[step, at], pass_sem.at[step, j], to)

        def passed_in(j):
            at = row_at(1 - core, lax.rem(z + 4 - j, 4))
            return remote(cross.at[step, at], cross.at[step, at], pass_sem.at[step, j], partner)

        for j in (2, 1, 3):
            gather(j).start()
            if j == 2:
                passed(2).start()
        passed(0).start()
        for j in (1, 3):
            gather_in(j).wait_recv()
            passed(j).start()
        gather_in(2).wait_recv()

        for j in range(1, 8):
            square_in(j).wait_recv()
        total = squares[step, 0]
        for k in range(1, 8):
            total = total + squares[step, k]
        left_scale = lax.rsqrt(total[:, :width] + EPSILON)
        right_scale = lax.rsqrt(total[:, width : 2 * width] + EPSILON)
        left_scale = jnp.broadcast_to(left_scale, (width, width)).T
        for j in range(4):
            passed_in(j).wait_recv()

        scaled = 0.5 * cross[step] * left_scale * right_scale
        scaled = scaled / (1.0 + jnp.sqrt(jnp.sum(scaled * scaled)))
        e = split(scaled)
        upper = polynomial(dot(e, e, (1, 1)), eye, g)
        lower = polynomial(dot(e, e, (0, 0)), eye, g)
        mixed = dot(split(upper), e)
        turned = -mixed.T
        chosen = jnp.concatenate([total[:, 2 * width :]] * (width // 128), axis=1) * 0.25
        flip = core.astype(jnp.float32) if step < STEPS - 1 else 0.0
        second_sent = (chosen * (1.0 - flip) + (1.0 - chosen) * flip) > 0.5
        for at, zero, one in (
            (slice(0, width), upper, mixed),
            (slice(width, 2 * width), turned, lower),
        ):
            kept_high, kept_low = split(jnp.where(second_sent, zero, one))
            sent_high, sent_low = split(jnp.where(second_sent, one, zero))
            weights_high[at, :width] = kept_high
            weights_high[at, width:] = sent_high
            weights_low[at, :width] = kept_low
            weights_low[at, width:] = sent_low

        if step > 0:

            @pl.loop(0, CHUNKS)
            def _(c):
                sent(step - 1, c).wait_send()

        @pl.loop(0, CHUNKS)
        def _(c):
            at = chunk_rows(c)
            high, low = split(jnp.concatenate([data[step, 0, at], data[step, 1, at]], axis=1))
            result = dot((high, low), (weights_high[...], weights_low[...]))
            if step < STEPS - 1:
                staged[0, at] = result[:, width:]
                sent(step, c).start()
                data[step + 1, core, at] = result[:, :width]
            else:
                staged[1, at] = result[:, width:]

                @pl.when(detours)
                def _():
                    moving_detour(c).start()

                @pl.when(jnp.logical_not(detours))
                def _():
                    moving_direct(c).start()

                staged[0, at] = result[:, :width]

                @pl.when(core == 0)
                def _():
                    staying_local(c).start()

                @pl.when(core == 1)
                def _():
                    staying_back(c).start()

        far_share(0).wait_send()
        far_share(1).wait_send()
        for j in (1, 3, 0):
            exchange(j).wait_send()
        for j in (1, 3):
            share(j).wait_send()
        for j in range(4):
            passed(j).wait_send()
        for j in (1, 2, 3):
            gather(j).wait_send()
        for j in range(1, 8):
            square(j).wait_send()

    @pl.when(relays)
    def _():
        @pl.loop(0, CHUNKS)
        def _(c):
            moving_detour(c).wait_recv()
            relay(c).start()

    @pl.loop(0, CHUNKS)
    def _(c):
        moving_direct(c).wait()

        @pl.when(relays)
        def _():
            relay(c).wait_send()

        @pl.when(core == 0)
        def _():
            staying_local(c).wait()

        @pl.when(core == 1)
        def _():
            staying_back(c).wait()


def body(snapshot, plan):
    rows, width = snapshot.shape[0], snapshot.shape[1] // 2
    quarter = width // 8
    dma = pltpu.SemaphoreType.DMA
    f32 = jnp.float32
    return pl.pallas_call(
        functools.partial(kernel, lax.axis_size("pairs")),
        out_shape=jax.ShapeDtypeStruct(snapshot.shape, f32),
        in_specs=[
            pl.BlockSpec(memory_space=pltpu.HBM),
            pl.BlockSpec(memory_space=pltpu.VMEM),
        ],
        out_specs=pl.BlockSpec(memory_space=pl.ANY),
        scratch_shapes=[
            pltpu.VMEM((STEPS, 2, rows, width), f32),
            pltpu.VMEM((2, rows, width), f32),
            pltpu.VMEM((rows, width), f32),
            pltpu.VMEM((STEPS, 8, 1, 2 * width + 128), f32),
            pltpu.VMEM((STEPS, width, width), f32),
            pltpu.VMEM((STEPS, 4, quarter, width), f32),
            pltpu.VMEM((STEPS, 4, quarter, width), f32),
            pltpu.VMEM((STEPS, 5, quarter, width), f32),
            pltpu.VMEM((STEPS, width, width), f32),
            pltpu.VMEM((2 * width, 2 * width), jnp.bfloat16),
            pltpu.VMEM((2 * width, 2 * width), jnp.bfloat16),
            dma((CHUNKS, 2)),
            dma((STEPS, 8, 2)),
            dma((STEPS, 4, 2)),
            dma((STEPS, 4, 2)),
            dma((STEPS, 4, 2)),
            dma((STEPS, 4, 2)),
            dma((STEPS, CHUNKS, 2)),
            dma((CHUNKS, 2)),
            dma((CHUNKS, 2)),
            dma((CHUNKS, 2)),
        ],
        compiler_params=pltpu.CompilerParams(
            collective_id=0, has_side_effects=True, vmem_limit_bytes=47 * 1024 * 1024
        ),
    )(snapshot, plan)


def solution(mesh):
    placed = (P("rows", "pairs"), P(None, "pairs"))
    return jax.shard_map(
        body, mesh=mesh, in_specs=placed, out_specs=P("rows", "pairs"), check_vma=False
    )
```

```python
import functools

import jax
import jax.numpy as jnp
from jax import lax
from jax.experimental import pallas as pl
from jax.experimental.pallas import tpu as pltpu
from jax.sharding import PartitionSpec as P
from numpy.polynomial import Polynomial

STEPS = 3
CHUNKS = 8
DIRECT = (1, 2)
LAG = 2
LINE = 4
EPSILON = 1e-06
MESH = pl.DeviceIdType.MESH


def gains():
    product = Polynomial([0.8, 0.8])
    first = 1.5 - 0.5 * product
    second = 1.5 - 0.5 * product * first * first
    return [float(c) for c in (first * second / 1.25**0.5).coef]


def split(x):
    high = x.astype(jnp.bfloat16)
    return high, (x - high.astype(jnp.float32)).astype(jnp.bfloat16)


def dot(a, b, dims=(1, 0)):
    def one(x, y):
        return lax.dot_general(
            x, y, (((dims[0],), (dims[1],)), ((), ())), preferred_element_type=jnp.float32
        )

    return one(a[0], b[0]) + (one(a[0], b[1]) + one(a[1], b[0]))


def polynomial(square, eye, g):
    s = split(square)
    square2 = dot(s, s)
    return (g[0] * eye + g[1] * square + g[2] * square2) + dot(
        split(square2), split(g[3] * square + g[4] * square2)
    )


def kernel(
    n_pairs,
    snapshot,
    plan,
    out,
    data,
    staged,
    relayed,
    squares,
    parted,
    partner_part,
    shares,
    arrived,
    cross,
    weights_high,
    weights_low,
    load_sem,
    square_sem,
    pair_sem,
    share_sem,
    gather_sem,
    pass_sem,
    block_sem,
    staying_sem,
    moving_sem,
    relay_sem,
):
    rows, width = snapshot.shape[0], snapshot.shape[1] // 2
    chunk, half, quarter = rows // CHUNKS, width // 2, width // 8
    r, p = lax.axis_index("rows"), lax.axis_index("pairs")
    core, z, x = lax.rem(r, 2), lax.div(r, 2), lax.rem(p, LINE)
    g = gains()

    def pair_at(distance):
        return lax.rem(p + distance + 2 * n_pairs, n_pairs)

    def chunk_rows(c):
        return pl.ds(pl.multiple_of(c * chunk, chunk), chunk)

    def row_at(c, z_index):
        return pl.ds(pl.multiple_of(c * half + z_index * quarter, quarter), quarter)

    def load(c, side):
        return pltpu.make_async_copy(
            snapshot.at[chunk_rows(c), pl.ds(side * width, width)],
            data.at[0, side, chunk_rows(c)],
            load_sem.at[c, side],
        )

    for c in range(CHUNKS):
        for side in range(2):
            load(c, side).start()

    barrier = pltpu.get_barrier_semaphore()
    peers = [(lax.rem(z + j, 4) * 2 + core, p) for j in (1, 2, 3)]
    peers += [(r, pair_at(d)) for d in (1, -1, 2, -2, 3, -3, 4, -4)]
    peers += [
        (lax.rem(z + j, 4) * 2 + 1 - core, pair_at(step * (2 * core - 1)))
        for j in range(4)
        for step in range(STEPS)
    ]
    for peer in peers:
        pl.semaphore_signal(barrier, inc=1, device_id=peer, device_id_type=MESH)

    def remote(src, dst, sems, device):
        return pltpu.make_async_remote_copy(
            src_ref=src,
            dst_ref=dst,
            send_sem=sems.at[0],
            recv_sem=sems.at[1],
            device_id=device,
            device_id_type=MESH,
        )

    eye = (
        lax.broadcasted_iota(jnp.int32, (width, width), 0)
        == lax.broadcasted_iota(jnp.int32, (width, width), 1)
    ).astype(jnp.float32)

    def sent(step, c):
        return remote(
            staged.at[0, chunk_rows(c)],
            data.at[step + 1, 1 - core, chunk_rows(c)],
            block_sem.at[step, c],
            (r, pair_at(1 - 2 * core)),
        )

    first_half, second_half = pl.ds(0, width), pl.ds(width, width)
    detours = jnp.where(core == 0, x == LINE - 1, x != 0)
    relays = jnp.where(core == 0, x == 0, x != 0)

    def staying_local(c):
        return pltpu.make_async_copy(
            staged.at[0, chunk_rows(c)], out.at[chunk_rows(c), first_half], staying_sem.at[c, 0]
        )

    def staying_back(c):
        return remote(
            staged.at[0, chunk_rows(c)],
            out.at[chunk_rows(c), first_half],
            staying_sem.at[c],
            (r, pair_at(2)),
        )

    def moving_direct(c):
        return remote(
            staged.at[1, chunk_rows(c)],
            out.at[chunk_rows(c), second_half],
            moving_sem.at[c],
            (r, pair_at(1 + 2 * core)),
        )

    def moving_detour(c):
        return pltpu.make_async_remote_copy(
            src_ref=staged.at[1, chunk_rows(c)],
            dst_ref=relayed.at[chunk_rows(c)],
            send_sem=moving_sem.at[c, 0],
            recv_sem=relay_sem.at[c, 1],
            device_id=(r, pair_at(7 * core - 3)),
            device_id_type=MESH,
        )

    def relay(c):
        return pltpu.make_async_remote_copy(
            src_ref=relayed.at[chunk_rows(c)],
            dst_ref=out.at[chunk_rows(c), second_half],
            send_sem=relay_sem.at[c, 0],
            recv_sem=moving_sem.at[c, 1],
            device_id=(r, pair_at(4 - 5 * core)),
            device_id_type=MESH,
        )

    for step in range(STEPS):
        parted[step] = jnp.zeros((width, width), jnp.float32)
        slot = z * 2 + core
        squares[step, slot] = jnp.zeros((1, 2 * width + 128), jnp.float32)

        @pl.loop(0, CHUNKS)
        def _(c):
            if step == 0:
                load(c, 0).wait()
                load(c, 1).wait()
            else:
                sent(step - 1, c).wait_recv()
            left = data[step, 0, chunk_rows(c)]
            right = data[step, 1, chunk_rows(c)]
            (left_high, left_low), (right_high, right_low) = split(left), split(right)
            parted[step] += lax.dot_general(
                jnp.concatenate([left_high, left_high, left_low], axis=0),
                jnp.concatenate([right_high, right_low, right_high], axis=0),
                (((0,), (0,)), ((), ())),
                preferred_element_type=jnp.float32,
            )
            squares[step, slot, :, :width] += jnp.sum(left * left, axis=0, keepdims=True)
            squares[step, slot, :, width : 2 * width] += jnp.sum(
                right * right, axis=0, keepdims=True
            )

        choice = plan[:, step : step + 1].astype(jnp.float32) * (1 - core).astype(jnp.float32)
        squares[step, slot, :, 2 * width :] = jnp.broadcast_to(choice, (1, 128))

        if step == 0:
            pl.semaphore_wait(barrier, len(peers))

        partner_pair = pair_at(step * (2 * core - 1))
        partner = (z * 2 + 1 - core, partner_pair)

        def exchange(j):
            k = lax.rem(z + j, 4)
            return remote(
                parted.at[step, row_at(1 - core, k)],
                partner_part.at[step, k],
                pair_sem.at[step, j],
                partner,
            )

        def square(j):
            other = lax.rem(slot + j, 8)
            same = lax.rem(other, 2) == core
            return remote(
                squares.at[step, slot],
                squares.at[step, slot],
                square_sem.at[step, j],
                (other, jnp.where(same, p, partner_pair)),
            )

        def square_in(j):
            at = squares.at[step, lax.rem(slot + 8 - j, 8)]
            return remote(at, at, square_sem.at[step, j], partner)

        far = lax.rem(z + 2, 4)

        def far_share(t):
            to = core if t == 0 else 1 - core
            return remote(
                parted.at[step, row_at(to, far)],
                arrived.at[step, z if t == 0 else 4],
                share_sem.at[step, 2 * t],
                (far * 2 + to, p if t == 0 else partner_pair),
            )

        def far_share_in(t):
            at = arrived.at[step, far if t == 0 else 4]
            return remote(at, at, share_sem.at[step, 2 * t], partner)

        far_share(0).start()
        far_share(1).start()
        for j in (1, 3, 0):
            exchange(j).start()
        for j in range(1, 8):
            square(j).start()

        def share(j):
            k = lax.rem(z + j, 4)
            return remote(
                shares.at[step, j], arrived.at[step, z], share_sem.at[step, j], (k * 2 + core, p)
            )

        def share_in(j):
            at = arrived.at[step, lax.rem(z + 4 - j, 4)]
            return remote(at, at, share_sem.at[step, j], partner)

        for j in (1, 3, 0):
            k = lax.rem(z + j, 4)
            exchange(j).wait_recv()
            own = parted[step, row_at(core, k)] + partner_part[step, k]
            if j:
                shares[step, j] = own
                share(j).start()
            else:
                arrived[step, k] = own
        for j in (1, 3):
            share_in(j).wait_recv()
        far_share_in(0).wait_recv()
        far_share_in(1).wait_recv()
        mine = row_at(core, z)
        cross[step, mine] = (arrived[step, 0] + arrived[step, 1]) + (
            (arrived[step, 2] + arrived[step, 3]) + arrived[step, 4]
        )

        def gather(j):
            return remote(
                cross.at[step, mine],
                cross.at[step, mine],
                gather_sem.at[step, j],
                (lax.rem(z + j, 4) * 2 + core, p),
            )

        def gather_in(j):
            at = row_at(core, lax.rem(z + 4 - j, 4))
            return remote(
                cross.at[step, at], cross.at[step, at], gather_sem.at[step, j], (r, pair_at(1))
            )

        def passed(j):
            direct = j == 2 or step in DIRECT
            at = row_at(core, z if direct else lax.rem(z + 4 - j, 4))
            to = (lax.rem(z + j, 4) * 2 + 1 - core, partner_pair) if direct else partner
            return remote(cross.at[step, at], cross.at[step, at], pass_sem.at[step, j], to)

        def passed_in(j):
            at = row_at(1 - core, lax.rem(z + 4 - j, 4))
            return remote(cross.at[step, at], cross.at[step, at], pass_sem.at[step, j], partner)

        for j in (2, 1, 3):
            gather(j).start()
            if j == 2 or step in DIRECT:
                passed(j).start()
        passed(0).start()
        for j in (1, 3):
            gather_in(j).wait_recv()
            if step not in DIRECT:
                passed(j).start()
        gather_in(2).wait_recv()

        for j in range(1, 8):
            square_in(j).wait_recv()
        total = squares[step, 0]
        for k in range(1, 8):
            total = total + squares[step, k]
        left_scale = lax.rsqrt(total[:, :width] + EPSILON)
        right_scale = lax.rsqrt(total[:, width : 2 * width] + EPSILON)
        left_scale = jnp.broadcast_to(left_scale, (width, width)).T
        for j in range(4):
            passed_in(j).wait_recv()

        scaled = 0.5 * cross[step] * left_scale * right_scale
        scaled = scaled / (1.0 + jnp.sqrt(jnp.sum(scaled * scaled)))
        e = split(scaled)
        upper = polynomial(dot(e, e, (1, 1)), eye, g)
        lower = polynomial(dot(e, e, (0, 0)), eye, g)
        mixed = dot(split(upper), e)
        turned = -mixed.T
        chosen = jnp.concatenate([total[:, 2 * width :]] * (width // 128), axis=1) * 0.25
        flip = core.astype(jnp.float32) if step < STEPS - 1 else 0.0
        second_sent = (chosen * (1.0 - flip) + (1.0 - chosen) * flip) > 0.5
        for at, zero, one in (
            (slice(0, width), upper, mixed),
            (slice(width, 2 * width), turned, lower),
        ):
            kept_high, kept_low = split(jnp.where(second_sent, zero, one))
            sent_high, sent_low = split(jnp.where(second_sent, one, zero))
            weights_high[at, :width] = kept_high
            weights_high[at, width:] = sent_high
            weights_low[at, :width] = kept_low
            weights_low[at, width:] = sent_low

        if step > 0:

            @pl.loop(0, CHUNKS)
            def _(c):
                sent(step - 1, c).wait_send()

        @pl.loop(0, CHUNKS)
        def _(c):
            at = chunk_rows(c)
            high, low = split(jnp.concatenate([data[step, 0, at], data[step, 1, at]], axis=1))
            result = dot((high, low), (weights_high[...], weights_low[...]))
            if step < STEPS - 1:
                staged[0, at] = result[:, width:]
                sent(step, c).start()
                data[step + 1, core, at] = result[:, :width]
            else:
                staged[1, at] = result[:, width:]

                @pl.when(detours)
                def _():
                    moving_detour(c).start()

                @pl.when(jnp.logical_not(detours))
                def _():
                    moving_direct(c).start()

                staged[0, at] = result[:, :width]

                @pl.when(core == 0)
                def _():
                    staying_local(c).start()

                @pl.when(core == 1)
                def _():
                    staying_back(c).start()

                @pl.when(jnp.logical_and(relays, c >= LAG))
                def _():
                    moving_detour(c - LAG).wait_recv()
                    relay(c - LAG).start()

        far_share(0).wait_send()
        far_share(1).wait_send()
        for j in (1, 3, 0):
            exchange(j).wait_send()
        for j in (1, 3):
            share(j).wait_send()
        for j in range(4):
            passed(j).wait_send()
        for j in (1, 2, 3):
            gather(j).wait_send()
        for j in range(1, 8):
            square(j).wait_send()

    @pl.when(relays)
    def _():
        @pl.loop(CHUNKS - LAG, CHUNKS)
        def _(c):
            moving_detour(c).wait_recv()
            relay(c).start()

    @pl.loop(0, CHUNKS)
    def _(c):
        moving_direct(c).wait()

        @pl.when(relays)
        def _():
            relay(c).wait_send()

        @pl.when(core == 0)
        def _():
            staying_local(c).wait()

        @pl.when(core == 1)
        def _():
            staying_back(c).wait()


def body(snapshot, plan):
    rows, width = snapshot.shape[0], snapshot.shape[1] // 2
    quarter = width // 8
    dma = pltpu.SemaphoreType.DMA
    f32 = jnp.float32
    return pl.pallas_call(
        functools.partial(kernel, lax.axis_size("pairs")),
        out_shape=jax.ShapeDtypeStruct(snapshot.shape, f32),
        in_specs=[
            pl.BlockSpec(memory_space=pltpu.HBM),
            pl.BlockSpec(memory_space=pltpu.VMEM),
        ],
        out_specs=pl.BlockSpec(memory_space=pl.ANY),
        scratch_shapes=[
            pltpu.VMEM((STEPS, 2, rows, width), f32),
            pltpu.VMEM((2, rows, width), f32),
            pltpu.VMEM((rows, width), f32),
            pltpu.VMEM((STEPS, 8, 1, 2 * width + 128), f32),
            pltpu.VMEM((STEPS, width, width), f32),
            pltpu.VMEM((STEPS, 4, quarter, width), f32),
            pltpu.VMEM((STEPS, 4, quarter, width), f32),
            pltpu.VMEM((STEPS, 5, quarter, width), f32),
            pltpu.VMEM((STEPS, width, width), f32),
            pltpu.VMEM((2 * width, 2 * width), jnp.bfloat16),
            pltpu.VMEM((2 * width, 2 * width), jnp.bfloat16),
            dma((CHUNKS, 2)),
            dma((STEPS, 8, 2)),
            dma((STEPS, 4, 2)),
            dma((STEPS, 4, 2)),
            dma((STEPS, 4, 2)),
            dma((STEPS, 4, 2)),
            dma((STEPS, CHUNKS, 2)),
            dma((CHUNKS, 2)),
            dma((CHUNKS, 2)),
            dma((CHUNKS, 2)),
        ],
        compiler_params=pltpu.CompilerParams(
            collective_id=0, has_side_effects=True, vmem_limit_bytes=47 * 1024 * 1024
        ),
    )(snapshot, plan.T)


def solution(mesh):
    placed = (P("rows", "pairs"), P(None, "pairs"))
    return jax.shard_map(
        body, mesh=mesh, in_specs=placed, out_specs=P("rows", "pairs"), check_vma=False
    )
```

```python
import functools

import jax
import jax.numpy as jnp
from jax import lax
from jax.experimental import pallas as pl
from jax.experimental.pallas import tpu as pltpu
from jax.sharding import PartitionSpec as P
from numpy.polynomial import Polynomial

STEPS = 3
CHUNKS = 8
RAW = (1, 2, 0)
PIECES = 4
PACE = (1, 2, 2, 3)
DIRECT = (1, 2)
LAG = 2
LINE = 4
EPSILON = 1e-06
MESH = pl.DeviceIdType.MESH


def gains():
    product = Polynomial([0.8, 0.8])
    first = 1.5 - 0.5 * product
    second = 1.5 - 0.5 * product * first * first
    return [float(c) for c in (first * second / 1.25**0.5).coef]


def split(x):
    high = x.astype(jnp.bfloat16)
    return high, (x - high.astype(jnp.float32)).astype(jnp.bfloat16)


def dot(a, b, dims=(1, 0)):
    def one(x, y):
        return lax.dot_general(
            x, y, (((dims[0],), (dims[1],)), ((), ())), preferred_element_type=jnp.float32
        )

    return one(a[0], b[0]) + (one(a[0], b[1]) + one(a[1], b[0]))


def turn(scaled, eye, g):
    e = split(scaled)
    upper = polynomial(dot(e, e, (1, 1)), eye, g)
    lower = polynomial(dot(e, e, (0, 0)), eye, g)
    mixed = dot(split(upper), e)
    return (upper, -mixed.T), (mixed, lower)


def polynomial(square, eye, g):
    s = split(square)
    square2 = dot(s, s)
    return (g[0] * eye + g[1] * square + g[2] * square2) + dot(
        split(square2), split(g[3] * square + g[4] * square2)
    )


def kernel(
    n_pairs,
    snapshot,
    plan,
    out,
    data,
    staged,
    relayed,
    raw,
    turned_out,
    turned_in,
    squares,
    parted,
    partner_part,
    shares,
    arrived,
    cross,
    weights_high,
    weights_low,
    load_sem,
    square_sem,
    pair_sem,
    share_sem,
    gather_sem,
    pass_sem,
    block_sem,
    staying_sem,
    moving_sem,
    relay_sem,
    raw_sem,
    turned_sem,
):
    rows, width = snapshot.shape[0], snapshot.shape[1] // 2
    chunk, half, quarter = rows // CHUNKS, width // 2, width // 8
    r, p = lax.axis_index("rows"), lax.axis_index("pairs")
    core, z, x = lax.rem(r, 2), lax.div(r, 2), lax.rem(p, LINE)
    g = gains()

    def pair_at(distance):
        return lax.rem(p + distance + 2 * n_pairs, n_pairs)

    def chunk_rows(c):
        return pl.ds(pl.multiple_of(c * chunk, chunk), chunk)

    def row_at(c, z_index):
        return pl.ds(pl.multiple_of(c * half + z_index * quarter, quarter), quarter)

    def load(c, side):
        return pltpu.make_async_copy(
            snapshot.at[chunk_rows(c), pl.ds(side * width, width)],
            data.at[0, side, chunk_rows(c)],
            load_sem.at[c, side],
        )

    for c in range(CHUNKS):
        for side in range(2):
            load(c, side).start()

    barrier = pltpu.get_barrier_semaphore()
    peers = [(lax.rem(z + j, 4) * 2 + core, p) for j in (1, 2, 3)]
    peers += [(r, pair_at(d)) for d in (1, -1, 2, -2, 3, -3, 4, -4)]
    peers += [
        (lax.rem(z + j, 4) * 2 + 1 - core, pair_at(step * (2 * core - 1)))
        for j in range(4)
        for step in range(STEPS)
    ]
    for peer in peers:
        pl.semaphore_signal(barrier, inc=1, device_id=peer, device_id_type=MESH)

    def remote(src, dst, sems, device):
        return pltpu.make_async_remote_copy(
            src_ref=src,
            dst_ref=dst,
            send_sem=sems.at[0],
            recv_sem=sems.at[1],
            device_id=device,
            device_id_type=MESH,
        )

    eye = (
        lax.broadcasted_iota(jnp.int32, (width, width), 0)
        == lax.broadcasted_iota(jnp.int32, (width, width), 1)
    ).astype(jnp.float32)

    piece = chunk // PIECES

    def raw_sent(step, i):
        start = (CHUNKS - RAW[step]) * chunk + i * piece
        return remote(
            data.at[step, :, pl.ds(start, piece)],
            raw.at[step, :, pl.ds(i * piece, piece)],
            raw_sem.at[step, i],
            (r, pair_at(1 - 2 * core)),
        )

    def start_raw(step, stage):
        total = RAW[step] * PIECES
        low = min(sum(PACE[:stage]), total)
        high = total if stage == 3 else min(sum(PACE[: stage + 1]), total)
        for i in range(low, high):
            raw_sent(step, i).start()

    def turned(step):
        return remote(
            turned_out.at[step],
            turned_in.at[step],
            turned_sem.at[step],
            (r, pair_at(1 - 2 * core)),
        )

    def sent(step, c):
        return remote(
            staged.at[0, chunk_rows(c)],
            data.at[step + 1, 1 - core, chunk_rows(c)],
            block_sem.at[step, c],
            (r, pair_at(1 - 2 * core)),
        )

    first_half, second_half = pl.ds(0, width), pl.ds(width, width)
    detours = jnp.where(core == 0, x == LINE - 1, x != 0)
    relays = jnp.where(core == 0, x == 0, x != 0)

    def staying_local(c):
        return pltpu.make_async_copy(
            staged.at[0, chunk_rows(c)], out.at[chunk_rows(c), first_half], staying_sem.at[c, 0]
        )

    def staying_back(c):
        return remote(
            staged.at[0, chunk_rows(c)],
            out.at[chunk_rows(c), first_half],
            staying_sem.at[c],
            (r, pair_at(2)),
        )

    def moving_direct(c):
        return remote(
            staged.at[1, chunk_rows(c)],
            out.at[chunk_rows(c), second_half],
            moving_sem.at[c],
            (r, pair_at(1 + 2 * core)),
        )

    def moving_detour(c):
        return pltpu.make_async_remote_copy(
            src_ref=staged.at[1, chunk_rows(c)],
            dst_ref=relayed.at[chunk_rows(c)],
            send_sem=moving_sem.at[c, 0],
            recv_sem=relay_sem.at[c, 1],
            device_id=(r, pair_at(7 * core - 3)),
            device_id_type=MESH,
        )

    def relay(c):
        return pltpu.make_async_remote_copy(
            src_ref=relayed.at[chunk_rows(c)],
            dst_ref=out.at[chunk_rows(c), second_half],
            send_sem=relay_sem.at[c, 0],
            recv_sem=moving_sem.at[c, 1],
            device_id=(r, pair_at(4 - 5 * core)),
            device_id_type=MESH,
        )

    for step in range(STEPS):
        parted[step] = jnp.zeros((width, width), jnp.float32)
        slot = z * 2 + core
        squares[step, slot] = jnp.zeros((1, 2 * width + 128), jnp.float32)

        def gram(c):
            left = data[step, 0, chunk_rows(c)]
            right = data[step, 1, chunk_rows(c)]
            (left_high, left_low), (right_high, right_low) = split(left), split(right)
            parted[step] += lax.dot_general(
                jnp.concatenate([left_high, left_high, left_low], axis=0),
                jnp.concatenate([right_high, right_low, right_high], axis=0),
                (((0,), (0,)), ((), ())),
                preferred_element_type=jnp.float32,
            )
            squares[step, slot, :, :width] += jnp.sum(left * left, axis=0, keepdims=True)
            squares[step, slot, :, width : 2 * width] += jnp.sum(
                right * right, axis=0, keepdims=True
            )

        if step == 0:

            @pl.loop(0, CHUNKS)
            def _(c):
                load(c, 0).wait()
                load(c, 1).wait()
                gram(c)
        else:
            pl.loop(CHUNKS - RAW[step - 1], CHUNKS)(gram)

            @pl.loop(0, CHUNKS - RAW[step - 1])
            def _(c):
                sent(step - 1, c).wait_recv()
                gram(c)

        choice = plan[:, step : step + 1].astype(jnp.float32) * (1 - core).astype(jnp.float32)
        squares[step, slot, :, 2 * width :] = jnp.broadcast_to(choice, (1, 128))

        if step == 0:
            pl.semaphore_wait(barrier, len(peers))

        partner_pair = pair_at(step * (2 * core - 1))
        partner = (z * 2 + 1 - core, partner_pair)

        def exchange(j):
            k = lax.rem(z + j, 4)
            return remote(
                parted.at[step, row_at(1 - core, k)],
                partner_part.at[step, k],
                pair_sem.at[step, j],
                partner,
            )

        def square(j):
            other = lax.rem(slot + j, 8)
            same = lax.rem(other, 2) == core
            return remote(
                squares.at[step, slot],
                squares.at[step, slot],
                square_sem.at[step, j],
                (other, jnp.where(same, p, partner_pair)),
            )

        def square_in(j):
            at = squares.at[step, lax.rem(slot + 8 - j, 8)]
            return remote(at, at, square_sem.at[step, j], partner)

        far = lax.rem(z + 2, 4)

        def far_share(t):
            to = core if t == 0 else 1 - core
            return remote(
                parted.at[step, row_at(to, far)],
                arrived.at[step, z if t == 0 else 4],
                share_sem.at[step, 2 * t],
                (far * 2 + to, p if t == 0 else partner_pair),
            )

        def far_share_in(t):
            at = arrived.at[step, far if t == 0 else 4]
            return remote(at, at, share_sem.at[step, 2 * t], partner)

        far_share(0).start()
        far_share(1).start()
        for j in (1, 3, 0):
            exchange(j).start()
        for j in range(1, 8):
            square(j).start()
        start_raw(step, 0)

        def share(j):
            k = lax.rem(z + j, 4)
            return remote(
                shares.at[step, j], arrived.at[step, z], share_sem.at[step, j], (k * 2 + core, p)
            )

        def share_in(j):
            at = arrived.at[step, lax.rem(z + 4 - j, 4)]
            return remote(at, at, share_sem.at[step, j], partner)

        for j in (1, 3, 0):
            k = lax.rem(z + j, 4)
            exchange(j).wait_recv()
            own = parted[step, row_at(core, k)] + partner_part[step, k]
            if j:
                shares[step, j] = own
                share(j).start()
            else:
                arrived[step, k] = own
        start_raw(step, 1)
        for j in (1, 3):
            share_in(j).wait_recv()
        far_share_in(0).wait_recv()
        far_share_in(1).wait_recv()
        mine = row_at(core, z)
        cross[step, mine] = (arrived[step, 0] + arrived[step, 1]) + (
            (arrived[step, 2] + arrived[step, 3]) + arrived[step, 4]
        )

        def gather(j):
            return remote(
                cross.at[step, mine],
                cross.at[step, mine],
                gather_sem.at[step, j],
                (lax.rem(z + j, 4) * 2 + core, p),
            )

        def gather_in(j):
            at = row_at(core, lax.rem(z + 4 - j, 4))
            return remote(
                cross.at[step, at], cross.at[step, at], gather_sem.at[step, j], (r, pair_at(1))
            )

        def passed(j):
            direct = j == 2 or step in DIRECT
            at = row_at(core, z if direct else lax.rem(z + 4 - j, 4))
            to = (lax.rem(z + j, 4) * 2 + 1 - core, partner_pair) if direct else partner
            return remote(cross.at[step, at], cross.at[step, at], pass_sem.at[step, j], to)

        def passed_in(j):
            at = row_at(1 - core, lax.rem(z + 4 - j, 4))
            return remote(cross.at[step, at], cross.at[step, at], pass_sem.at[step, j], partner)

        for j in (2, 1, 3):
            gather(j).start()
            if j == 2 or step in DIRECT:
                passed(j).start()
        passed(0).start()
        start_raw(step, 2)
        for j in (1, 3):
            gather_in(j).wait_recv()
            if step not in DIRECT:
                passed(j).start()
        start_raw(step, 3)
        gather_in(2).wait_recv()

        for j in range(1, 8):
            square_in(j).wait_recv()
        total = squares[step, 0]
        for k in range(1, 8):
            total = total + squares[step, k]
        left_scale = lax.rsqrt(total[:, :width] + EPSILON)
        right_scale = lax.rsqrt(total[:, width : 2 * width] + EPSILON)
        left_scale = jnp.broadcast_to(left_scale, (width, width)).T
        for j in range(4):
            passed_in(j).wait_recv()

        scaled = 0.5 * cross[step] * left_scale * right_scale
        scaled = scaled / (1.0 + jnp.sqrt(jnp.sum(scaled * scaled)))
        chosen = jnp.concatenate([total[:, 2 * width :]] * (width // 128), axis=1) * 0.25
        flip = core.astype(jnp.float32) if step < STEPS - 1 else 0.0
        second_sent = chosen * (1.0 - flip) + (1.0 - chosen) * flip
        if step < STEPS - 1:
            turned_out[step, :width] = scaled
            turned_out[step, width:] = jnp.broadcast_to(second_sent, (8, width))
            turned(step).start()
        zero, one = turn(scaled, eye, g)

        def put(side, pick, zero, one):
            for k in range(2):
                at = slice(k * width, (k + 1) * width), slice(side * width, (side + 1) * width)
                weights_high[at], weights_low[at] = split(jnp.where(pick > 0.5, one[k], zero[k]))

        put(0, 1.0 - second_sent, zero, one)
        put(1, second_sent, zero, one)

        if step > 0:

            @pl.loop(0, CHUNKS - RAW[step - 1])
            def _(c):
                sent(step - 1, c).wait_send()

        @pl.loop(0, CHUNKS)
        def _(c):
            at = chunk_rows(c)
            high, low = split(jnp.concatenate([data[step, 0, at], data[step, 1, at]], axis=1))
            result = dot((high, low), (weights_high[...], weights_low[...]))
            if step < STEPS - 1:
                staged[0, at] = result[:, width:]
                data[step + 1, core, at] = result[:, :width]

                @pl.when(c < CHUNKS - RAW[step])
                def _():
                    sent(step, c).start()
            else:
                staged[1, at] = result[:, width:]

                @pl.when(detours)
                def _():
                    moving_detour(c).start()

                @pl.when(jnp.logical_not(detours))
                def _():
                    moving_direct(c).start()

                staged[0, at] = result[:, :width]

                @pl.when(core == 0)
                def _():
                    staying_local(c).start()

                @pl.when(core == 1)
                def _():
                    staying_back(c).start()

                @pl.when(jnp.logical_and(relays, c >= LAG))
                def _():
                    moving_detour(c - LAG).wait_recv()
                    relay(c - LAG).start()

        if step < STEPS - 1:
            turned(step).wait_recv()
            zero, one = turn(turned_in[step, :width], eye, g)
            put(1, turned_in[step, width : width + 1], zero, one)
            for i in range(RAW[step] * PIECES):
                raw_sent(step, i).wait_recv()

            @pl.loop(0, RAW[step])
            def _(i):
                at = chunk_rows(i)
                high, low = split(jnp.concatenate([raw[step, 0, at], raw[step, 1, at]], axis=1))
                data[step + 1, 1 - core, chunk_rows(i + CHUNKS - RAW[step])] = dot(
                    (high, low), (weights_high[:, width:], weights_low[:, width:])
                )

            turned(step).wait_send()
            for i in range(RAW[step] * PIECES):
                raw_sent(step, i).wait_send()

        far_share(0).wait_send()
        far_share(1).wait_send()
        for j in (1, 3, 0):
            exchange(j).wait_send()
        for j in (1, 3):
            share(j).wait_send()
        for j in range(4):
            passed(j).wait_send()
        for j in (1, 2, 3):
            gather(j).wait_send()
        for j in range(1, 8):
            square(j).wait_send()

    @pl.when(relays)
    def _():
        @pl.loop(CHUNKS - LAG, CHUNKS)
        def _(c):
            moving_detour(c).wait_recv()
            relay(c).start()

    @pl.loop(0, CHUNKS)
    def _(c):
        moving_direct(c).wait()

        @pl.when(relays)
        def _():
            relay(c).wait_send()

        @pl.when(core == 0)
        def _():
            staying_local(c).wait()

        @pl.when(core == 1)
        def _():
            staying_back(c).wait()


def body(snapshot, plan):
    rows, width = snapshot.shape[0], snapshot.shape[1] // 2
    quarter = width // 8
    dma = pltpu.SemaphoreType.DMA
    f32 = jnp.float32
    return pl.pallas_call(
        functools.partial(kernel, lax.axis_size("pairs")),
        out_shape=jax.ShapeDtypeStruct(snapshot.shape, f32),
        in_specs=[
            pl.BlockSpec(memory_space=pltpu.HBM),
            pl.BlockSpec(memory_space=pltpu.VMEM),
        ],
        out_specs=pl.BlockSpec(memory_space=pl.ANY),
        scratch_shapes=[
            pltpu.VMEM((STEPS, 2, rows, width), f32),
            pltpu.VMEM((2, rows, width), f32),
            pltpu.VMEM((rows, width), f32),
            pltpu.VMEM((STEPS - 1, 2, max(RAW) * rows // CHUNKS, width), f32),
            pltpu.VMEM((STEPS - 1, width + 8, width), f32),
            pltpu.VMEM((STEPS - 1, width + 8, width), f32),
            pltpu.VMEM((STEPS, 8, 1, 2 * width + 128), f32),
            pltpu.VMEM((STEPS, width, width), f32),
            pltpu.VMEM((STEPS, 4, quarter, width), f32),
            pltpu.VMEM((STEPS, 4, quarter, width), f32),
            pltpu.VMEM((STEPS, 5, quarter, width), f32),
            pltpu.VMEM((STEPS, width, width), f32),
            pltpu.VMEM((2 * width, 2 * width), jnp.bfloat16),
            pltpu.VMEM((2 * width, 2 * width), jnp.bfloat16),
            dma((CHUNKS, 2)),
            dma((STEPS, 8, 2)),
            dma((STEPS, 4, 2)),
            dma((STEPS, 4, 2)),
            dma((STEPS, 4, 2)),
            dma((STEPS, 4, 2)),
            dma((STEPS, CHUNKS, 2)),
            dma((CHUNKS, 2)),
            dma((CHUNKS, 2)),
            dma((CHUNKS, 2)),
            dma((STEPS, max(RAW) * PIECES, 2)),
            dma((STEPS, 2)),
        ],
        compiler_params=pltpu.CompilerParams(
            collective_id=0, has_side_effects=True, vmem_limit_bytes=47 * 1024 * 1024
        ),
    )(snapshot, plan.T)


def solution(mesh):
    placed = (P("rows", "pairs"), P(None, "pairs"))
    return jax.shard_map(
        body, mesh=mesh, in_specs=placed, out_specs=P("rows", "pairs"), check_vma=False
    )
```

```python
import functools

import jax
import jax.numpy as jnp
from jax import lax
from jax.experimental import pallas as pl
from jax.experimental.pallas import tpu as pltpu
from jax.sharding import PartitionSpec as P
from numpy.polynomial import Polynomial

STEPS = 3
CHUNKS = 8
DIRECT = (1, 2)
LAG = 2
LINE = 4
EPSILON = 1e-06
MESH = pl.DeviceIdType.MESH


def gains():
    product = Polynomial([0.8, 0.8])
    first = 1.5 - 0.5 * product
    second = 1.5 - 0.5 * product * first * first
    return [float(c) for c in (first * second / 1.25**0.5).coef]


def split(x):
    high = x.astype(jnp.bfloat16)
    return high, (x - high.astype(jnp.float32)).astype(jnp.bfloat16)


def dot(a, b, dims=(1, 0)):
    def one(x, y):
        return lax.dot_general(
            x, y, (((dims[0],), (dims[1],)), ((), ())), preferred_element_type=jnp.float32
        )

    return one(a[0], b[0]) + (one(a[0], b[1]) + one(a[1], b[0]))


def polynomial(square, eye, g):
    s = split(square)
    square2 = dot(s, s)
    return (g[0] * eye + g[1] * square + g[2] * square2) + dot(
        split(square2), split(g[3] * square + g[4] * square2)
    )


def kernel(
    n_pairs,
    snapshot,
    plan,
    out,
    data,
    staged,
    relayed,
    squares,
    parted,
    partner_part,
    shares,
    arrived,
    cross,
    weights_high,
    weights_low,
    load_sem,
    square_sem,
    pair_sem,
    share_sem,
    gather_sem,
    pass_sem,
    block_sem,
    staying_sem,
    moving_sem,
    relay_sem,
):
    rows, width = snapshot.shape[0], snapshot.shape[1] // 2
    chunk, half, quarter = rows // CHUNKS, width // 2, width // 8
    r, p = lax.axis_index("rows"), lax.axis_index("pairs")
    core, z, x = lax.rem(r, 2), lax.div(r, 2), lax.rem(p, LINE)
    g = gains()

    def pair_at(distance):
        return lax.rem(p + distance + 2 * n_pairs, n_pairs)

    def chunk_rows(c):
        return pl.ds(pl.multiple_of(c * chunk, chunk), chunk)

    def row_at(c, z_index):
        return pl.ds(pl.multiple_of(c * half + z_index * quarter, quarter), quarter)

    def load(c, side):
        return pltpu.make_async_copy(
            snapshot.at[chunk_rows(c), pl.ds(side * width, width)],
            data.at[0, side, chunk_rows(c)],
            load_sem.at[c, side],
        )

    for c in range(CHUNKS):
        for side in range(2):
            load(c, side).start()

    barrier = pltpu.get_barrier_semaphore()
    peers = [(lax.rem(z + j, 4) * 2 + core, p) for j in (1, 2, 3)]
    peers += [(r, pair_at(d)) for d in (1, -1, 2, -2, 3, -3, 4, -4)]
    peers += [
        (lax.rem(z + j, 4) * 2 + 1 - core, pair_at(step * (2 * core - 1)))
        for j in range(4)
        for step in range(STEPS)
    ]
    for peer in peers:
        pl.semaphore_signal(barrier, inc=1, device_id=peer, device_id_type=MESH)

    def remote(src, dst, sems, device):
        return pltpu.make_async_remote_copy(
            src_ref=src,
            dst_ref=dst,
            send_sem=sems.at[0],
            recv_sem=sems.at[1],
            device_id=device,
            device_id_type=MESH,
        )

    eye = (
        lax.broadcasted_iota(jnp.int32, (width, width), 0)
        == lax.broadcasted_iota(jnp.int32, (width, width), 1)
    ).astype(jnp.float32)

    def sent(step, c):
        return remote(
            staged.at[0, chunk_rows(c)],
            data.at[step + 1, 1 - core, chunk_rows(c)],
            block_sem.at[step, c],
            (r, pair_at(1 - 2 * core)),
        )

    first_half, second_half = pl.ds(0, width), pl.ds(width, width)
    detours = jnp.where(core == 0, x == LINE - 1, x != 0)
    relays = jnp.where(core == 0, x == 0, x != 0)

    def staying_local(c):
        return pltpu.make_async_copy(
            staged.at[0, chunk_rows(c)], out.at[chunk_rows(c), first_half], staying_sem.at[c, 0]
        )

    def staying_back(c):
        return remote(
            staged.at[0, chunk_rows(c)],
            out.at[chunk_rows(c), first_half],
            staying_sem.at[c],
            (r, pair_at(2)),
        )

    def moving_direct(c):
        return remote(
            staged.at[1, chunk_rows(c)],
            out.at[chunk_rows(c), second_half],
            moving_sem.at[c],
            (r, pair_at(1 + 2 * core)),
        )

    def moving_detour(c):
        return pltpu.make_async_remote_copy(
            src_ref=staged.at[1, chunk_rows(c)],
            dst_ref=relayed.at[chunk_rows(c)],
            send_sem=moving_sem.at[c, 0],
            recv_sem=relay_sem.at[c, 1],
            device_id=(r, pair_at(7 * core - 3)),
            device_id_type=MESH,
        )

    def relay(c):
        return pltpu.make_async_remote_copy(
            src_ref=relayed.at[chunk_rows(c)],
            dst_ref=out.at[chunk_rows(c), second_half],
            send_sem=relay_sem.at[c, 0],
            recv_sem=moving_sem.at[c, 1],
            device_id=(r, pair_at(4 - 5 * core)),
            device_id_type=MESH,
        )

    for step in range(STEPS):
        parted[step] = jnp.zeros((width, width), jnp.float32)
        slot = z * 2 + core
        squares[step, slot] = jnp.zeros((1, 2 * width + 128), jnp.float32)

        @pl.loop(0, CHUNKS)
        def _(c):
            if step == 0:
                load(c, 0).wait()
                load(c, 1).wait()
            else:
                sent(step - 1, c).wait_recv()
            left = data[step, 0, chunk_rows(c)]
            right = data[step, 1, chunk_rows(c)]
            (left_high, left_low), (right_high, right_low) = split(left), split(right)
            parted[step] += lax.dot_general(
                jnp.concatenate([left_high, left_high, left_low], axis=0),
                jnp.concatenate([right_high, right_low, right_high], axis=0),
                (((0,), (0,)), ((), ())),
                preferred_element_type=jnp.float32,
            )
            squares[step, slot, :, :width] += jnp.sum(left * left, axis=0, keepdims=True)
            squares[step, slot, :, width : 2 * width] += jnp.sum(
                right * right, axis=0, keepdims=True
            )

        choice = plan[:, step : step + 1].astype(jnp.float32) * (1 - core).astype(jnp.float32)
        squares[step, slot, :, 2 * width :] = jnp.broadcast_to(choice, (1, 128))

        if step == 0:
            pl.semaphore_wait(barrier, len(peers))

        partner_pair = pair_at(step * (2 * core - 1))
        partner = (z * 2 + 1 - core, partner_pair)

        def exchange(j):
            k = lax.rem(z + j, 4)
            return remote(
                parted.at[step, row_at(1 - core, k)],
                partner_part.at[step, k],
                pair_sem.at[step, j],
                partner,
            )

        def square(j):
            other = lax.rem(slot + j, 8)
            same = lax.rem(other, 2) == core
            return remote(
                squares.at[step, slot],
                squares.at[step, slot],
                square_sem.at[step, j],
                (other, jnp.where(same, p, partner_pair)),
            )

        def square_in(j):
            at = squares.at[step, lax.rem(slot + 8 - j, 8)]
            return remote(at, at, square_sem.at[step, j], partner)

        far = lax.rem(z + 2, 4)

        def far_share(t):
            to = core if t == 0 else 1 - core
            return remote(
                parted.at[step, row_at(to, far)],
                arrived.at[step, z if t == 0 else 4],
                share_sem.at[step, 2 * t],
                (far * 2 + to, p if t == 0 else partner_pair),
            )

        def far_share_in(t):
            at = arrived.at[step, far if t == 0 else 4]
            return remote(at, at, share_sem.at[step, 2 * t], partner)

        def straight(t, j):
            k, to = lax.rem(z + j, 4), core if t == 0 else 1 - core
            return remote(
                parted.at[step, row_at(to, k)],
                arrived.at[step, z + 4 * t],
                (share_sem if t == 0 else pair_sem).at[step, j],
                (k * 2 + to, p if t == 0 else partner_pair),
            )

        def straight_in(t, j):
            at = arrived.at[step, lax.rem(z + 4 - j, 4) + 4 * t]
            return remote(at, at, (share_sem if t == 0 else pair_sem).at[step, j], partner)

        ways = ((0, 2), (1, 2), (0, 1), (0, 3), (1, 1), (1, 3), (1, 0))
        if step in DIRECT:
            for t, j in ways:
                straight(t, j).start()
        else:
            far_share(0).start()
            far_share(1).start()
            for j in (1, 3, 0):
                exchange(j).start()
        for j in range(1, 8):
            square(j).start()

        def share(j):
            k = lax.rem(z + j, 4)
            return remote(
                shares.at[step, j], arrived.at[step, z], share_sem.at[step, j], (k * 2 + core, p)
            )

        def share_in(j):
            at = arrived.at[step, lax.rem(z + 4 - j, 4)]
            return remote(at, at, share_sem.at[step, j], partner)

        mine = row_at(core, z)
        if step in DIRECT:
            total = parted[step, mine]
            for t, j in ways[::-1]:
                straight_in(t, j).wait_recv()
                total = total + arrived[step, lax.rem(z + 4 - j, 4) + 4 * t]
            cross[step, mine] = total
        else:
            for j in (1, 3, 0):
                k = lax.rem(z + j, 4)
                exchange(j).wait_recv()
                own = parted[step, row_at(core, k)] + partner_part[step, k]
                if j:
                    shares[step, j] = own
                    share(j).start()
                else:
                    arrived[step, k] = own
            for j in (1, 3):
                share_in(j).wait_recv()
            far_share_in(0).wait_recv()
            far_share_in(1).wait_recv()
            cross[step, mine] = (arrived[step, 0] + arrived[step, 1]) + (
                (arrived[step, 2] + arrived[step, 3]) + arrived[step, 4]
            )

        def gather(j):
            return remote(
                cross.at[step, mine],
                cross.at[step, mine],
                gather_sem.at[step, j],
                (lax.rem(z + j, 4) * 2 + core, p),
            )

        def gather_in(j):
            at = row_at(core, lax.rem(z + 4 - j, 4))
            return remote(
                cross.at[step, at], cross.at[step, at], gather_sem.at[step, j], (r, pair_at(1))
            )

        def passed(j):
            direct = j == 2 or step in DIRECT
            at = row_at(core, z if direct else lax.rem(z + 4 - j, 4))
            to = (lax.rem(z + j, 4) * 2 + 1 - core, partner_pair) if direct else partner
            return remote(cross.at[step, at], cross.at[step, at], pass_sem.at[step, j], to)

        def passed_in(j):
            at = row_at(1 - core, lax.rem(z + 4 - j, 4))
            return remote(cross.at[step, at], cross.at[step, at], pass_sem.at[step, j], partner)

        for j in (2, 1, 3):
            gather(j).start()
            if j == 2 or step in DIRECT:
                passed(j).start()
        passed(0).start()
        for j in (1, 3):
            gather_in(j).wait_recv()
            if step not in DIRECT:
                passed(j).start()
        gather_in(2).wait_recv()

        for j in range(1, 8):
            square_in(j).wait_recv()
        total = squares[step, 0]
        for k in range(1, 8):
            total = total + squares[step, k]
        left_scale = lax.rsqrt(total[:, :width] + EPSILON)
        right_scale = lax.rsqrt(total[:, width : 2 * width] + EPSILON)
        left_scale = jnp.broadcast_to(left_scale, (width, width)).T
        for j in range(4):
            passed_in(j).wait_recv()

        scaled = 0.5 * cross[step] * left_scale * right_scale
        scaled = scaled / (1.0 + jnp.sqrt(jnp.sum(scaled * scaled)))
        e = split(scaled)
        upper = polynomial(dot(e, e, (1, 1)), eye, g)
        lower = polynomial(dot(e, e, (0, 0)), eye, g)
        mixed = dot(split(upper), e)
        turned = -mixed.T
        chosen = jnp.concatenate([total[:, 2 * width :]] * (width // 128), axis=1) * 0.25
        flip = core.astype(jnp.float32) if step < STEPS - 1 else 0.0
        second_sent = (chosen * (1.0 - flip) + (1.0 - chosen) * flip) > 0.5
        for at, zero, one in (
            (slice(0, width), upper, mixed),
            (slice(width, 2 * width), turned, lower),
        ):
            kept_high, kept_low = split(jnp.where(second_sent, zero, one))
            sent_high, sent_low = split(jnp.where(second_sent, one, zero))
            weights_high[at, :width] = kept_high
            weights_high[at, width:] = sent_high
            weights_low[at, :width] = kept_low
            weights_low[at, width:] = sent_low

        if step > 0:

            @pl.loop(0, CHUNKS)
            def _(c):
                sent(step - 1, c).wait_send()

        @pl.loop(0, CHUNKS)
        def _(c):
            at = chunk_rows(c)
            high, low = split(jnp.concatenate([data[step, 0, at], data[step, 1, at]], axis=1))
            result = dot((high, low), (weights_high[...], weights_low[...]))
            if step < STEPS - 1:
                staged[0, at] = result[:, width:]
                sent(step, c).start()
                data[step + 1, core, at] = result[:, :width]
            else:
                staged[1, at] = result[:, width:]

                @pl.when(detours)
                def _():
                    moving_detour(c).start()

                @pl.when(jnp.logical_not(detours))
                def _():
                    moving_direct(c).start()

                staged[0, at] = result[:, :width]

                @pl.when(core == 0)
                def _():
                    staying_local(c).start()

                @pl.when(core == 1)
                def _():
                    staying_back(c).start()

                @pl.when(jnp.logical_and(relays, c >= LAG))
                def _():
                    moving_detour(c - LAG).wait_recv()
                    relay(c - LAG).start()

        if step in DIRECT:
            for t, j in ways:
                straight(t, j).wait_send()
        else:
            far_share(0).wait_send()
            far_share(1).wait_send()
            for j in (1, 3, 0):
                exchange(j).wait_send()
            for j in (1, 3):
                share(j).wait_send()
        for j in range(4):
            passed(j).wait_send()
        for j in (1, 2, 3):
            gather(j).wait_send()
        for j in range(1, 8):
            square(j).wait_send()

    @pl.when(relays)
    def _():
        @pl.loop(CHUNKS - LAG, CHUNKS)
        def _(c):
            moving_detour(c).wait_recv()
            relay(c).start()

    @pl.loop(0, CHUNKS)
    def _(c):
        moving_direct(c).wait()

        @pl.when(relays)
        def _():
            relay(c).wait_send()

        @pl.when(core == 0)
        def _():
            staying_local(c).wait()

        @pl.when(core == 1)
        def _():
            staying_back(c).wait()


def body(snapshot, plan):
    rows, width = snapshot.shape[0], snapshot.shape[1] // 2
    quarter = width // 8
    dma = pltpu.SemaphoreType.DMA
    f32 = jnp.float32
    return pl.pallas_call(
        functools.partial(kernel, lax.axis_size("pairs")),
        out_shape=jax.ShapeDtypeStruct(snapshot.shape, f32),
        in_specs=[
            pl.BlockSpec(memory_space=pltpu.HBM),
            pl.BlockSpec(memory_space=pltpu.VMEM),
        ],
        out_specs=pl.BlockSpec(memory_space=pl.ANY),
        scratch_shapes=[
            pltpu.VMEM((STEPS, 2, rows, width), f32),
            pltpu.VMEM((2, rows, width), f32),
            pltpu.VMEM((rows, width), f32),
            pltpu.VMEM((STEPS, 8, 1, 2 * width + 128), f32),
            pltpu.VMEM((STEPS, width, width), f32),
            pltpu.VMEM((STEPS, 4, quarter, width), f32),
            pltpu.VMEM((STEPS, 4, quarter, width), f32),
            pltpu.VMEM((STEPS, 8, quarter, width), f32),
            pltpu.VMEM((STEPS, width, width), f32),
            pltpu.VMEM((2 * width, 2 * width), jnp.bfloat16),
            pltpu.VMEM((2 * width, 2 * width), jnp.bfloat16),
            dma((CHUNKS, 2)),
            dma((STEPS, 8, 2)),
            dma((STEPS, 4, 2)),
            dma((STEPS, 4, 2)),
            dma((STEPS, 4, 2)),
            dma((STEPS, 4, 2)),
            dma((STEPS, CHUNKS, 2)),
            dma((CHUNKS, 2)),
            dma((CHUNKS, 2)),
            dma((CHUNKS, 2)),
        ],
        compiler_params=pltpu.CompilerParams(
            collective_id=0, has_side_effects=True, vmem_limit_bytes=47 * 1024 * 1024
        ),
    )(snapshot, plan.T)


def solution(mesh):
    placed = (P("rows", "pairs"), P(None, "pairs"))
    return jax.shard_map(
        body, mesh=mesh, in_specs=placed, out_specs=P("rows", "pairs"), check_vma=False
    )
```

```python
import functools

import jax
import jax.numpy as jnp
from jax import lax
from jax.experimental import pallas as pl
from jax.experimental.pallas import tpu as pltpu
from jax.sharding import PartitionSpec as P
from numpy.polynomial import Polynomial

STEPS = 3
CHUNKS = 8
DIRECT = (1, 2)
LAG = 3
LINE = 4
EPSILON = 1e-06
MESH = pl.DeviceIdType.MESH


def gains():
    product = Polynomial([0.8, 0.8])
    first = 1.5 - 0.5 * product
    second = 1.5 - 0.5 * product * first * first
    return [float(c) for c in (first * second / 1.25**0.5).coef]


def split(x):
    high = x.astype(jnp.bfloat16)
    return high, (x - high.astype(jnp.float32)).astype(jnp.bfloat16)


def dot(a, b, dims=(1, 0)):
    def one(x, y):
        return lax.dot_general(
            x, y, (((dims[0],), (dims[1],)), ((), ())), preferred_element_type=jnp.float32
        )

    return one(a[0], b[0]) + (one(a[0], b[1]) + one(a[1], b[0]))


def polynomial(square, eye, g):
    s = split(square)
    square2 = dot(s, s)
    return (g[0] * eye + g[1] * square + g[2] * square2) + dot(
        split(square2), split(g[3] * square + g[4] * square2)
    )


def kernel(
    n_pairs,
    snapshot,
    plan,
    out,
    data,
    staged,
    relayed,
    squares,
    parted,
    partner_part,
    shares,
    arrived,
    cross,
    weights_high,
    weights_low,
    load_sem,
    square_sem,
    pair_sem,
    share_sem,
    gather_sem,
    pass_sem,
    block_sem,
    staying_sem,
    moving_sem,
    relay_sem,
):
    rows, width = snapshot.shape[0], snapshot.shape[1] // 2
    chunk, half, quarter = rows // CHUNKS, width // 2, width // 8
    r, p = lax.axis_index("rows"), lax.axis_index("pairs")
    core, z, x = lax.rem(r, 2), lax.div(r, 2), lax.rem(p, LINE)
    g = gains()

    def pair_at(distance):
        return lax.rem(p + distance + 2 * n_pairs, n_pairs)

    def chunk_rows(c):
        return pl.ds(pl.multiple_of(c * chunk, chunk), chunk)

    def row_at(c, z_index):
        return pl.ds(pl.multiple_of(c * half + z_index * quarter, quarter), quarter)

    def load(c, side):
        return pltpu.make_async_copy(
            snapshot.at[chunk_rows(c), pl.ds(side * width, width)],
            data.at[0, side, chunk_rows(c)],
            load_sem.at[c, side],
        )

    for c in range(CHUNKS):
        for side in range(2):
            load(c, side).start()

    barrier = pltpu.get_barrier_semaphore()
    peers = [(lax.rem(z + j, 4) * 2 + core, p) for j in (1, 2, 3)]
    peers += [(r, pair_at(d)) for d in (1, -1, 2, -2, 3, -3, 4, -4)]
    peers += [
        (lax.rem(z + j, 4) * 2 + 1 - core, pair_at(step * (2 * core - 1)))
        for j in range(4)
        for step in range(STEPS)
    ]
    for peer in peers:
        pl.semaphore_signal(barrier, inc=1, device_id=peer, device_id_type=MESH)

    def remote(src, dst, sems, device):
        return pltpu.make_async_remote_copy(
            src_ref=src,
            dst_ref=dst,
            send_sem=sems.at[0],
            recv_sem=sems.at[1],
            device_id=device,
            device_id_type=MESH,
        )

    eye = (
        lax.broadcasted_iota(jnp.int32, (width, width), 0)
        == lax.broadcasted_iota(jnp.int32, (width, width), 1)
    ).astype(jnp.float32)

    def sent(step, c):
        return remote(
            staged.at[0, chunk_rows(c)],
            data.at[step + 1, 1 - core, chunk_rows(c)],
            block_sem.at[step, c],
            (r, pair_at(1 - 2 * core)),
        )

    first_half, second_half = pl.ds(0, width), pl.ds(width, width)
    detours = jnp.where(core == 0, x == LINE - 1, x != 0)
    relays = jnp.where(core == 0, x == 0, x != 0)

    def staying_local(c):
        return pltpu.make_async_copy(
            staged.at[0, chunk_rows(c)], out.at[chunk_rows(c), first_half], staying_sem.at[c, 0]
        )

    def staying_back(c):
        return remote(
            staged.at[0, chunk_rows(c)],
            out.at[chunk_rows(c), first_half],
            staying_sem.at[c],
            (r, pair_at(2)),
        )

    def moving_direct(c):
        return remote(
            staged.at[1, chunk_rows(c)],
            out.at[chunk_rows(c), second_half],
            moving_sem.at[c],
            (r, pair_at(1 + 2 * core)),
        )

    def moving_detour(c):
        return pltpu.make_async_remote_copy(
            src_ref=staged.at[1, chunk_rows(c)],
            dst_ref=relayed.at[chunk_rows(c)],
            send_sem=moving_sem.at[c, 0],
            recv_sem=relay_sem.at[c, 1],
            device_id=(r, pair_at(7 * core - 3)),
            device_id_type=MESH,
        )

    def relay(c):
        return pltpu.make_async_remote_copy(
            src_ref=relayed.at[chunk_rows(c)],
            dst_ref=out.at[chunk_rows(c), second_half],
            send_sem=relay_sem.at[c, 0],
            recv_sem=moving_sem.at[c, 1],
            device_id=(r, pair_at(4 - 5 * core)),
            device_id_type=MESH,
        )

    for step in range(STEPS):
        parted[step] = jnp.zeros((width, width), jnp.float32)
        slot = z * 2 + core
        squares[step, slot] = jnp.zeros((1, 2 * width + 128), jnp.float32)

        @pl.loop(0, CHUNKS)
        def _(c):
            if step == 0:
                load(c, 0).wait()
                load(c, 1).wait()
            else:
                sent(step - 1, c).wait_recv()
            left = data[step, 0, chunk_rows(c)]
            right = data[step, 1, chunk_rows(c)]
            (left_high, left_low), (right_high, right_low) = split(left), split(right)
            parted[step] += lax.dot_general(
                jnp.concatenate([left_high, left_high, left_low], axis=0),
                jnp.concatenate([right_high, right_low, right_high], axis=0),
                (((0,), (0,)), ((), ())),
                preferred_element_type=jnp.float32,
            )
            squares[step, slot, :, :width] += jnp.sum(left * left, axis=0, keepdims=True)
            squares[step, slot, :, width : 2 * width] += jnp.sum(
                right * right, axis=0, keepdims=True
            )

        choice = plan[:, step : step + 1].astype(jnp.float32) * (1 - core).astype(jnp.float32)
        squares[step, slot, :, 2 * width :] = jnp.broadcast_to(choice, (1, 128))

        if step == 0:
            pl.semaphore_wait(barrier, len(peers))

        partner_pair = pair_at(step * (2 * core - 1))
        partner = (z * 2 + 1 - core, partner_pair)

        def exchange(j):
            k = lax.rem(z + j, 4)
            return remote(
                parted.at[step, row_at(1 - core, k)],
                partner_part.at[step, k],
                pair_sem.at[step, j],
                partner,
            )

        def square(j):
            other = lax.rem(slot + j, 8)
            same = lax.rem(other, 2) == core
            return remote(
                squares.at[step, slot],
                squares.at[step, slot],
                square_sem.at[step, j],
                (other, jnp.where(same, p, partner_pair)),
            )

        def square_in(j):
            at = squares.at[step, lax.rem(slot + 8 - j, 8)]
            return remote(at, at, square_sem.at[step, j], partner)

        far = lax.rem(z + 2, 4)

        def far_share(t):
            to = core if t == 0 else 1 - core
            return remote(
                parted.at[step, row_at(to, far)],
                arrived.at[step, z if t == 0 else 4],
                share_sem.at[step, 2 * t],
                (far * 2 + to, p if t == 0 else partner_pair),
            )

        def far_share_in(t):
            at = arrived.at[step, far if t == 0 else 4]
            return remote(at, at, share_sem.at[step, 2 * t], partner)

        def straight(t, j):
            k, to = lax.rem(z + j, 4), core if t == 0 else 1 - core
            return remote(
                parted.at[step, row_at(to, k)],
                arrived.at[step, z + 4 * t],
                (share_sem if t == 0 else pair_sem).at[step, j],
                (k * 2 + to, p if t == 0 else partner_pair),
            )

        def straight_in(t, j):
            at = arrived.at[step, lax.rem(z + 4 - j, 4) + 4 * t]
            return remote(at, at, (share_sem if t == 0 else pair_sem).at[step, j], partner)

        ways = ((0, 2), (1, 2), (0, 1), (0, 3), (1, 1), (1, 3), (1, 0))
        if step in DIRECT:
            for t, j in ways:
                straight(t, j).start()
        else:
            far_share(0).start()
            far_share(1).start()
            for j in (1, 3, 0):
                exchange(j).start()
        for j in range(1, 8):
            square(j).start()

        def share(j):
            k = lax.rem(z + j, 4)
            return remote(
                shares.at[step, j], arrived.at[step, z], share_sem.at[step, j], (k * 2 + core, p)
            )

        def share_in(j):
            at = arrived.at[step, lax.rem(z + 4 - j, 4)]
            return remote(at, at, share_sem.at[step, j], partner)

        mine = row_at(core, z)
        if step in DIRECT:
            total = parted[step, mine]
            for t, j in ways[::-1]:
                straight_in(t, j).wait_recv()
                total = total + arrived[step, lax.rem(z + 4 - j, 4) + 4 * t]
            cross[step, mine] = total
        else:
            for j in (1, 3, 0):
                k = lax.rem(z + j, 4)
                exchange(j).wait_recv()
                own = parted[step, row_at(core, k)] + partner_part[step, k]
                if j:
                    shares[step, j] = own
                    share(j).start()
                else:
                    arrived[step, k] = own
            for j in (1, 3):
                share_in(j).wait_recv()
            far_share_in(0).wait_recv()
            far_share_in(1).wait_recv()
            cross[step, mine] = (arrived[step, 0] + arrived[step, 1]) + (
                (arrived[step, 2] + arrived[step, 3]) + arrived[step, 4]
            )

        def gather(j):
            return remote(
                cross.at[step, mine],
                cross.at[step, mine],
                gather_sem.at[step, j],
                (lax.rem(z + j, 4) * 2 + core, p),
            )

        def gather_in(j):
            at = row_at(core, lax.rem(z + 4 - j, 4))
            return remote(
                cross.at[step, at], cross.at[step, at], gather_sem.at[step, j], (r, pair_at(1))
            )

        def passed(j):
            direct = j == 2 or step in DIRECT
            at = row_at(core, z if direct else lax.rem(z + 4 - j, 4))
            to = (lax.rem(z + j, 4) * 2 + 1 - core, partner_pair) if direct else partner
            return remote(cross.at[step, at], cross.at[step, at], pass_sem.at[step, j], to)

        def passed_in(j):
            at = row_at(1 - core, lax.rem(z + 4 - j, 4))
            return remote(cross.at[step, at], cross.at[step, at], pass_sem.at[step, j], partner)

        for j in (2, 1, 3):
            gather(j).start()
            if j == 2 or step in DIRECT:
                passed(j).start()
        passed(0).start()
        for j in (1, 3):
            gather_in(j).wait_recv()
            if step not in DIRECT:
                passed(j).start()
        gather_in(2).wait_recv()

        for j in range(1, 8):
            square_in(j).wait_recv()
        total = squares[step, 0]
        for k in range(1, 8):
            total = total + squares[step, k]
        left_scale = lax.rsqrt(total[:, :width] + EPSILON)
        right_scale = lax.rsqrt(total[:, width : 2 * width] + EPSILON)
        left_scale = jnp.broadcast_to(left_scale, (width, width)).T
        for j in range(4):
            passed_in(j).wait_recv()

        scaled = 0.5 * cross[step] * left_scale * right_scale
        scaled = scaled / (1.0 + jnp.sqrt(jnp.sum(scaled * scaled)))
        e = split(scaled)
        upper = polynomial(dot(e, e, (1, 1)), eye, g)
        lower = polynomial(dot(e, e, (0, 0)), eye, g)
        mixed = dot(split(upper), e)
        turned = -mixed.T
        chosen = jnp.concatenate([total[:, 2 * width :]] * (width // 128), axis=1) * 0.25
        flip = core.astype(jnp.float32) if step < STEPS - 1 else 0.0
        second_sent = (chosen * (1.0 - flip) + (1.0 - chosen) * flip) > 0.5
        for at, zero, one in (
            (slice(0, width), upper, mixed),
            (slice(width, 2 * width), turned, lower),
        ):
            kept_high, kept_low = split(jnp.where(second_sent, zero, one))
            sent_high, sent_low = split(jnp.where(second_sent, one, zero))
            weights_high[at, :width] = kept_high
            weights_high[at, width:] = sent_high
            weights_low[at, :width] = kept_low
            weights_low[at, width:] = sent_low

        if step > 0:

            @pl.loop(0, CHUNKS)
            def _(c):
                sent(step - 1, c).wait_send()

        @pl.loop(0, CHUNKS)
        def _(c):
            at = chunk_rows(c)
            high, low = split(jnp.concatenate([data[step, 0, at], data[step, 1, at]], axis=1))
            result = dot((high, low), (weights_high[...], weights_low[...]))
            if step < STEPS - 1:
                staged[0, at] = result[:, width:]
                sent(step, c).start()
                data[step + 1, core, at] = result[:, :width]
            else:
                staged[1, at] = result[:, width:]

                @pl.when(detours)
                def _():
                    moving_detour(c).start()

                @pl.when(jnp.logical_not(detours))
                def _():
                    moving_direct(c).start()

                staged[0, at] = result[:, :width]

                @pl.when(core == 0)
                def _():
                    staying_local(c).start()

                @pl.when(core == 1)
                def _():
                    staying_back(c).start()

                @pl.when(jnp.logical_and(relays, c >= LAG))
                def _():
                    moving_detour(c - LAG).wait_recv()
                    relay(c - LAG).start()

        if step in DIRECT:
            for t, j in ways:
                straight(t, j).wait_send()
        else:
            far_share(0).wait_send()
            far_share(1).wait_send()
            for j in (1, 3, 0):
                exchange(j).wait_send()
            for j in (1, 3):
                share(j).wait_send()
        for j in range(4):
            passed(j).wait_send()
        for j in (1, 2, 3):
            gather(j).wait_send()
        for j in range(1, 8):
            square(j).wait_send()

    @pl.when(relays)
    def _():
        @pl.loop(CHUNKS - LAG, CHUNKS)
        def _(c):
            moving_detour(c).wait_recv()
            relay(c).start()

    @pl.loop(0, CHUNKS)
    def _(c):
        moving_direct(c).wait()

        @pl.when(relays)
        def _():
            relay(c).wait_send()

        @pl.when(core == 0)
        def _():
            staying_local(c).wait()

        @pl.when(core == 1)
        def _():
            staying_back(c).wait()


def body(snapshot, plan):
    rows, width = snapshot.shape[0], snapshot.shape[1] // 2
    quarter = width // 8
    dma = pltpu.SemaphoreType.DMA
    f32 = jnp.float32
    return pl.pallas_call(
        functools.partial(kernel, lax.axis_size("pairs")),
        out_shape=jax.ShapeDtypeStruct(snapshot.shape, f32),
        in_specs=[
            pl.BlockSpec(memory_space=pltpu.HBM),
            pl.BlockSpec(memory_space=pltpu.VMEM),
        ],
        out_specs=pl.BlockSpec(memory_space=pl.ANY),
        scratch_shapes=[
            pltpu.VMEM((STEPS, 2, rows, width), f32),
            pltpu.VMEM((2, rows, width), f32),
            pltpu.VMEM((rows, width), f32),
            pltpu.VMEM((STEPS, 8, 1, 2 * width + 128), f32),
            pltpu.VMEM((STEPS, width, width), f32),
            pltpu.VMEM((STEPS, 4, quarter, width), f32),
            pltpu.VMEM((STEPS, 4, quarter, width), f32),
            pltpu.VMEM((STEPS, 8, quarter, width), f32),
            pltpu.VMEM((STEPS, width, width), f32),
            pltpu.VMEM((2 * width, 2 * width), jnp.bfloat16),
            pltpu.VMEM((2 * width, 2 * width), jnp.bfloat16),
            dma((CHUNKS, 2)),
            dma((STEPS, 8, 2)),
            dma((STEPS, 4, 2)),
            dma((STEPS, 4, 2)),
            dma((STEPS, 4, 2)),
            dma((STEPS, 4, 2)),
            dma((STEPS, CHUNKS, 2)),
            dma((CHUNKS, 2)),
            dma((CHUNKS, 2)),
            dma((CHUNKS, 2)),
        ],
        compiler_params=pltpu.CompilerParams(
            collective_id=0, has_side_effects=True, vmem_limit_bytes=47 * 1024 * 1024
        ),
    )(snapshot, plan.T)


def solution(mesh):
    placed = (P("rows", "pairs"), P(None, "pairs"))
    return jax.shard_map(
        body, mesh=mesh, in_specs=placed, out_specs=P("rows", "pairs"), check_vma=False
    )
```
